128 devices in a mesh: dp: 32 (over z, x, core), tensor: 4 (over y).
Axes of the slice: x: 4, y: 4, z: 4, core: 2. Of those that a mesh axis runs over, the one named last changes fastest.
Arguments:
- activations: bfloat16 [16384, 4096], P('dp'), may hold values from -6 to 6
- gate_up_grads: bfloat16 [2, 16384, 11008], P(None, 'dp', 'tensor'), may hold values from -60 to 60
- hidden_act: bfloat16 [16384, 11008], P('dp', 'tensor'), may hold values from -60 to 60
- down_out_grad: bfloat16 [16384, 4096], P('dp'), may hold values from -6 to 6
- bases: bfloat16 [3, 4096, 512], replicated, may hold values from -0.25 to 0.25
- first_moment: float32 [3, 4, 2752, 512], P(None, 'tensor', 'dp'), may hold values from -6 to 6
- second_moment: float32 [3, 4, 2752, 512], P(None, 'tensor', 'dp'), may hold values from 0.05 to 2
Outputs:
- gate_update: bfloat16 [4096, 11008], P('dp', 'tensor')
- up_update: bfloat16 [4096, 11008], P('dp', 'tensor')
- down_update: bfloat16 [11008, 4096], P('tensor', 'dp')
- new_first: float32 [3, 4, 2752, 512], P(None, 'tensor', 'dp')
- new_second: float32 [3, 4, 2752, 512], P(None, 'tensor', 'dp')
The draws below stay inside these ranges and needn't reach their ends.
All inputs are finite; a program needn't handle non-finite values.
Results may differ from the reference program's by a relative error of at most 0.013.
Values may be sent and summed in bfloat16 or wider, within the bound.
No kernel may reach another device: no remote copies, remote signals or barrier semaphores. Data moves between devices by JAX's collectives and lax.ppermute only.
A program may use at most 192 MiB of HBM per device.

```python
import math
import jax
import jax.numpy as jnp
from jax import lax

D = 4096
FF = 11008
R = 512
STEP = 10
TOK_DEV = 512
TOKENS = 16384
TSPLIT = 4
FF_T = 2752
N_DP = 32


def column_scales(key, column_count):
    ramp = 10.0 ** (jnp.arange(column_count, dtype=jnp.float32) / column_count)
    jitter = jnp.exp(jax.random.uniform(key, (column_count,), jnp.float32, -0.35, 0.35))
    return ramp * jitter


def unit_means(key, leading, column_count):
    subkeys = jax.random.split(key, 2)
    levels = jnp.exp(jax.random.uniform(subkeys[0], (leading, 64), jnp.float32, math.log(0.1), math.log(8.0)))
    position = jnp.arange(column_count, dtype=jnp.int32) * 64 // column_count
    weights = levels[:, position]
    signs = jax.random.rademacher(subkeys[1], (leading, column_count), jnp.float32)
    return signs * jnp.sqrt(weights * 3.0 / TOKENS)


def feature_rows(key, mean_scale):
    subkeys = jax.random.split(key, 2)
    means = mean_scale * jax.random.truncated_normal(subkeys[0], -2.5, 2.5, (1, D), jnp.float32)
    values = jax.random.truncated_normal(subkeys[1], -5.0, 5.0, (TOKENS, D), jnp.float32)
    return (0.8 * values + means).astype(jnp.bfloat16)


def draw_activations(key, part):
    key = jax.random.fold_in(key, 31)
    return feature_rows(key, 0.6)


def draw_down_out_grad(key, part):
    key = jax.random.fold_in(key, 37)
    return feature_rows(key, 0.6)


def draw_gate_up_grads(key, part):
    key = jax.random.fold_in(key, 11)
    subkeys = jax.random.split(key, 4)
    scales = column_scales(subkeys[0], FF)
    values = jax.random.truncated_normal(subkeys[1], -5.0, 5.0, (2, TOKENS, FF), jnp.float32)
    values = values + unit_means(subkeys[3], 2, FF)[:, None, :]
    return (0.3 * values * scales).astype(jnp.bfloat16)


def draw_hidden_act(key, part):
    key = jax.random.fold_in(key, 23)
    subkeys = jax.random.split(key, 4)
    scales = column_scales(subkeys[0], FF)
    values = jax.random.truncated_normal(subkeys[1], -5.0, 5.0, (TOKENS, FF), jnp.float32)
    values = values + unit_means(subkeys[3], 1, FF)
    return (0.3 * values * scales).astype(jnp.bfloat16)


def level_of(rng, dims, cuts, least, high):
    factor_of, own = 1.0, jax.random.fold_in(rng, 6)
    for axis_at, shards_of in cuts:
        steps = jnp.exp(jax.random.uniform(jax.random.fold_in(own, axis_at), (shards_of,), jnp.float32, least / len(cuts), high / len(cuts)))
        factor_of = factor_of * jnp.repeat(steps, dims[axis_at] // shards_of).reshape([-1 if axis == axis_at else 1 for axis in range(len(dims))])
    return factor_of


def scatter_about(key, dims, deviation, reach, cuts=(), kind=jnp.bfloat16):
    array = jax.random.normal(key, dims, jnp.float32) * deviation
    if len(cuts) > 0:
        array = level_of(key, dims, cuts, -0.22, 0.18) * array
    return jnp.clip(array, min=-reach, max=reach).astype(kind)


def setup_inputs(seed: int = 0) -> dict:
    key_list = jax.random.split(jax.random.key(seed), 8)
    activations = draw_activations(jax.random.fold_in(key_list[7], 71), 0)
    gate_up_grads = draw_gate_up_grads(jax.random.fold_in(key_list[7], 71), 0)
    hidden_act = draw_hidden_act(jax.random.fold_in(key_list[7], 71), 0)
    down_out_grad = draw_down_out_grad(jax.random.fold_in(key_list[7], 71), 0)
    bases = scatter_about(key_list[4], (3, D, R), R ** -0.5, 0.25)
    first_moment = scatter_about(key_list[5], (3, TSPLIT, FF_T, R), 1.0, 6.0, ((1, 4), (2, 32)), jnp.float32)
    second_moment = jnp.clip(jnp.exp(math.log(2.0) - 3.6888794 * jax.random.uniform(key_list[6], (3, TSPLIT, FF_T, R), jnp.float32) ** level_of(key_list[6], (3, TSPLIT, FF_T, R), ((1, 4), (2, 32)), -0.2, 0.2)), 0.05, 2.0)
    return dict(activations=activations, gate_up_grads=gate_up_grads, hidden_act=hidden_act, down_out_grad=down_out_grad, bases=bases, first_moment=first_moment, second_moment=second_moment)


def reference(activations, gate_up_grads, hidden_act, down_out_grad, bases, first_moment, second_moment):
    block_inputs = activations.reshape(N_DP, TOK_DEV, D)
    block_grads = gate_up_grads.reshape(2, N_DP, TOK_DEV, FF).transpose(1, 0, 2, 3)
    block_hidden = hidden_act.reshape(N_DP, TOK_DEV, FF)
    block_down = down_out_grad.reshape(N_DP, TOK_DEV, D)

    def accumulate(total, blocks):
        inputs, out_grads, hidden, down_grad = blocks
        terms = []
        for matrix_index in range(2):
            reduced = jnp.dot(inputs, bases[matrix_index], preferred_element_type=jnp.float32).astype(jnp.bfloat16)
            terms.append(jnp.dot(out_grads[matrix_index].T, reduced, preferred_element_type=jnp.float32))
        reduced = jnp.dot(down_grad, bases[2], preferred_element_type=jnp.float32).astype(jnp.bfloat16)
        terms.append(jnp.dot(hidden.T, reduced, preferred_element_type=jnp.float32))
        return (total + jnp.stack(terms), None)
    projected, _ = lax.scan(accumulate, jnp.zeros((3, FF, R), jnp.float32), (block_inputs, block_grads, block_hidden, block_down))
    clip_limit = jnp.sqrt(jnp.float32(3 * R * FF))
    factor = jnp.minimum(jnp.float32(1.0), clip_limit / jnp.sqrt(jnp.sum(projected * projected)))
    clipped = projected * factor
    moment_one = 0.9 * first_moment.reshape(3, FF, R) + 0.1 * clipped
    moment_two = 0.95 * second_moment.reshape(3, FF, R) + 0.05 * clipped * clipped
    direction = (moment_one / (1.0 - 0.9 ** STEP) / (jnp.sqrt(moment_two / (1.0 - 0.95 ** STEP)) + 1e-08)).astype(jnp.bfloat16)
    gate_update = jnp.dot(bases[0], direction[0].T, preferred_element_type=jnp.float32).astype(jnp.bfloat16)
    up_update = jnp.dot(bases[1], direction[1].T, preferred_element_type=jnp.float32).astype(jnp.bfloat16)
    down_update = jnp.dot(direction[2], bases[2].T, preferred_element_type=jnp.float32).astype(jnp.bfloat16)
    return (gate_update, up_update, down_update, moment_one.reshape(first_moment.shape), moment_two.reshape(second_moment.shape))
```

```python
import functools

import jax
import jax.numpy as jnp
from jax import lax
from jax.experimental import pallas as pl
from jax.experimental.pallas import tpu as pltpu
from jax.sharding import PartitionSpec as P

STEP = 10
N_Z, N_X, N_C = 4, 4, 2
N_DP = N_Z * N_X * N_C
UNITS = 86
PAD = 88
LANES = 128
BF16 = jnp.bfloat16
F32 = jnp.float32
MB = 1 << 20


def dp_index(z, x, c):
    return ((z % N_Z) * N_X + (x % N_X)) * N_C + c % N_C


def every_chip():
    return [(z, x, c) for z in range(N_Z) for x in range(N_X) for c in range(N_C)]


CORE_PAIRS = [(dp_index(z, x, c), dp_index(z, x, c + 1)) for z, x, c in every_chip()]


def along_x(s):
    return [(dp_index(z, x, c), dp_index(z, x + s, c)) for z, x, c in every_chip()]


def along_z(s):
    return [(dp_index(z, x, c), dp_index(z + s, x, c)) for z, x, c in every_chip()]


VMEM = pl.BlockSpec(memory_space=pltpu.VMEM)
SMEM = pl.BlockSpec(memory_space=pltpu.SMEM)


def params(mib, **more):
    return pltpu.CompilerParams(vmem_limit_bytes=mib * MB, **more)


def project_kernel(place, a_ref, b_ref, g_ref, keep_ref, send_ref, acc, terms):
    k = pl.program_id(0)
    part = jnp.dot(a_ref[...], b_ref[0], preferred_element_type=F32)

    @pl.when(k == 0)
    def _():
        acc[...] = part

    @pl.when(k > 0)
    def _():
        acc[...] += part

    @pl.when(k == pl.num_programs(0) - 1)
    def _():
        z0, x0, c0 = place[0], place[1], place[2]
        half = 2 * LANES
        mine = acc[:, pl.ds(pl.multiple_of(c0 * half, half), half)].astype(BF16)
        other = acc[:, pl.ds(pl.multiple_of((1 - c0) * half, half), half)].astype(BF16)
        reduced = jnp.concatenate([mine, other], axis=1)
        units = g_ref.shape[-1]

        def rows(at, count):
            g = g_ref[0, :, pl.ds(at, count)]
            terms[pl.ds(at, count), :] = lax.dot_general(
                g, reduced, (((0,), (0,)), ((), ())), preferred_element_type=F32
            )

        block = 256
        whole = units // block

        @pl.loop(0, whole)
        def _(j):
            rows(pl.multiple_of(j * block, block), block)

        if units % block:
            rows(whole * block, units % block)
        terms[units:, :] = jnp.zeros((terms.shape[0] - units, terms.shape[1]), F32)

        for z in range(N_Z):
            for x in range(N_X):
                sz = lax.rem(z - z0 + N_Z, N_Z)
                sx = lax.rem(x - x0 + N_X, N_X)
                for c in range(N_C):
                    own = lax.rem(c + c0, 2)
                    at = dp_index(z, x, c) * UNITS
                    chunk = terms[at : at + PAD, :].astype(BF16)
                    keep_ref[0, sx, sz, own] = chunk[:, 0:128]
                    keep_ref[1, sz, sx, own] = chunk[:, 128:256]
                    send_ref[0, sx, sz, 1 - own] = chunk[:, 256:384]
                    send_ref[1, sz, sx, 1 - own] = chunk[:, 384:512]


def project(place, a, bases, matrix, g, g_at):
    tokens, width = a.shape
    rank = bases.shape[2]
    units = g.shape[2]
    steps = 8
    wide = width // steps
    shape = (2, 4, 4, N_C, PAD, LANES)
    whole = pl.BlockSpec(shape, lambda k, s: (0,) * 6)
    return pl.pallas_call(
        project_kernel,
        grid_spec=pltpu.PrefetchScalarGridSpec(
            num_scalar_prefetch=1,
            grid=(steps,),
            in_specs=[
                pl.BlockSpec((tokens, wide), lambda k, s: (0, k)),
                pl.BlockSpec((1, wide, rank), lambda k, s: (matrix, k, 0)),
                pl.BlockSpec((1, tokens, units), lambda k, s: (g_at, 0, 0)),
            ],
            out_specs=[whole, whole],
            scratch_shapes=[
                pltpu.VMEM((tokens, rank), F32),
                pltpu.VMEM((N_DP * UNITS + 8, rank), F32),
            ],
        ),
        out_shape=[jax.ShapeDtypeStruct(shape, BF16)] * 2,
        compiler_params=params(40),
        cost_estimate=pl.CostEstimate(
            flops=2 * tokens * rank * (width + units),
            bytes_accessed=2 * (tokens * width + width * rank + tokens * units + units * rank),
            transcendentals=0,
        ),
        name="project",
    )(place, a, bases, g)


def pair_kernel(*refs):
    keep, recv, outs = refs[0:3], refs[3:6], refs[6:]
    step = pl.program_id(0)
    for i, out in enumerate(outs):

        @pl.when(step == i)
        def _(out=out):
            for m in range(3):
                out[:, m] = (keep[m][0].astype(F32) + recv[m][0].astype(F32)).astype(BF16)


def pair_sum(keep, recv):
    flat = [t.reshape(8, 4, N_C, PAD, LANES) for t in (*keep, *recv)]
    shape = (4, 3, N_C, PAD, LANES)
    return pl.pallas_call(
        pair_kernel,
        grid=(8,),
        in_specs=[pl.BlockSpec((1, 4, N_C, PAD, LANES), lambda i: (i, 0, 0, 0, 0))] * 6,
        out_specs=[pl.BlockSpec(shape, lambda i: (0,) * 5)] * 8,
        out_shape=[jax.ShapeDtypeStruct(shape, BF16)] * 8,
        compiler_params=params(32),
        name="pair_sum",
    )(*flat)


def stage_kernel(own, r1, r2, r3, *outs):
    for i, out in enumerate(outs):
        total = own[i].astype(F32) + r1[i].astype(F32)
        total = total + (r2[i].astype(F32) + r3[i].astype(F32))
        out[...] = total.astype(BF16)


def stage_sum(terms):
    shape = terms[0].shape[1:]
    return pl.pallas_call(
        stage_kernel,
        in_specs=[VMEM] * 4,
        out_specs=[VMEM] * 4,
        out_shape=[jax.ShapeDtypeStruct(shape, BF16)] * 4,
        compiler_params=params(16),
        name="stage_sum",
    )(*terms)


def owned_kernel(*refs):
    parts, (mine, fix, squares) = refs[:8], refs[8:]
    inside = lax.broadcasted_iota(jnp.int32, (PAD, LANES), 0) < UNITS
    total_sq = jnp.zeros((PAD, LANES), F32)
    for half in range(2):
        t = parts[4 * half : 4 * half + 4]
        lanes = slice(half * LANES, half * LANES + LANES)
        for m in range(3):
            for c in range(N_C):
                v = t[0][m, c].astype(F32) + t[1][m, c].astype(F32)
                v = v + (t[2][m, c].astype(F32) + t[3][m, c].astype(F32))
                total_sq += jnp.where(inside, v * v, 0.0)
                if c == 0:
                    mine[m, :, lanes] = v
                else:
                    fix[m, :, lanes] = v.astype(BF16)
    row = jnp.sum(total_sq, axis=0, keepdims=True)
    squares[...] = jnp.broadcast_to(row, squares.shape)


def owned_sum(first, second, peers):
    return pl.pallas_call(
        owned_kernel,
        in_specs=[VMEM] * 8,
        out_specs=[VMEM] * 3,
        out_shape=[
            jax.ShapeDtypeStruct((3, PAD, 2 * LANES), F32),
            jax.ShapeDtypeStruct((3, PAD, 2 * LANES), BF16),
            jax.ShapeDtypeStruct((peers, LANES), F32),
        ],
        compiler_params=params(16),
        name="owned_sum",
    )(*first, *second)


def adam_kernel(limit_sq, place, squares, mine, recv, first, second, new_first, new_second, direction):
    total = jnp.sum(squares[...])
    clip_limit = jnp.sqrt(jnp.full((1, 1), limit_sq, F32))
    factor = jnp.minimum(1.0, clip_limit / jnp.sqrt(jnp.full((1, 1), total, F32)))
    low = place[2] == 0
    for m in range(3):
        here = mine[m]
        there = recv[m].astype(F32)
        lower = jnp.where(low, here, there)
        upper = jnp.where(low, there, here)
        clipped = jnp.concatenate([lower, upper], axis=1)[:UNITS] * factor
        one = 0.9 * first[m] + 0.1 * clipped
        two = 0.95 * second[m] + 0.05 * clipped * clipped
        new_first[m] = one
        new_second[m] = two
        way = one / (1.0 - 0.9**STEP) / (jnp.sqrt(two / (1.0 - 0.95**STEP)) + 1e-08)
        padded = jnp.concatenate([way, jnp.zeros((PAD - UNITS, way.shape[1]), F32)], axis=0)
        direction[m] = padded.astype(BF16)


def adam(limit_sq, place, squares, mine, recv, first, second):
    rank = first.shape[-1]
    moment = jax.ShapeDtypeStruct((3, UNITS, rank), F32)
    return pl.pallas_call(
        functools.partial(adam_kernel, limit_sq),
        in_specs=[SMEM] + [VMEM] * 5,
        out_specs=[VMEM] * 3,
        out_shape=[moment, moment, jax.ShapeDtypeStruct((3, PAD, rank), BF16)],
        compiler_params=params(16),
        name="adam",
    )(place, squares, mine, recv, first, second)


def update_kernel(way, bases, out):
    for m in range(3):
        full = lax.dot_general(
            way[m], bases[m], (((1,), (1,)), ((), ())), preferred_element_type=F32
        ).astype(BF16)
        for j in range(out.shape[0]):
            out[j, m] = full[:, j * LANES : (j + 1) * LANES]


def updates(way, bases):
    width, rank = bases.shape[1:]
    wide = 512
    shape = (width // LANES, 3, PAD, LANES)
    return pl.pallas_call(
        update_kernel,
        grid=(width // wide,),
        in_specs=[
            pl.BlockSpec((3, PAD, rank), lambda i: (0, 0, 0)),
            pl.BlockSpec((3, wide, rank), lambda i: (0, i, 0)),
        ],
        out_specs=pl.BlockSpec((wide // LANES, 3, PAD, LANES), lambda i: (i, 0, 0, 0)),
        out_shape=jax.ShapeDtypeStruct(shape, BF16),
        compiler_params=params(24),
        name="updates",
    )(way, bases)


def layout_kernel(pieces, gate, up, down, rows):
    units = N_DP * UNITS
    for m, out in enumerate((gate, up, down)):
        for k in range(N_DP):
            rows[k * UNITS : k * UNITS + PAD, :] = pieces[k, m].astype(F32)
        if m == 2:
            out[...] = rows[:units, :].astype(BF16)
            continue
        for at in range(0, units, LANES):
            count = min(LANES, units - at)
            out[:, at : at + count] = rows[at : at + count, :].T.astype(BF16)


def layout(pieces):
    units = N_DP * UNITS
    return pl.pallas_call(
        layout_kernel,
        in_specs=[VMEM],
        out_specs=[VMEM] * 3,
        out_shape=[
            jax.ShapeDtypeStruct((LANES, units), BF16),
            jax.ShapeDtypeStruct((LANES, units), BF16),
            jax.ShapeDtypeStruct((units, LANES), BF16),
        ],
        scratch_shapes=[pltpu.VMEM((units + 8, LANES), F32)],
        compiler_params=params(24),
        name="layout",
    )(pieces)


def body(activations, gate_up_grads, hidden_act, down_out_grad, bases, first_moment, second_moment):
    devices = lax.axis_size("dp") * lax.axis_size("tensor")
    total_units = hidden_act.shape[1] * lax.axis_size("tensor")
    me = lax.axis_index("dp")
    place = jnp.stack([me // (N_X * N_C), (me // N_C) % N_X, me % N_C]).astype(jnp.int32)

    keep, recv = [], []
    for m, (a, g, at) in enumerate(
        (
            (activations, gate_up_grads, 0),
            (activations, gate_up_grads, 1),
            (down_out_grad, hidden_act[None], 0),
        )
    ):
        kept, sent = project(place, a, bases, m, g, at)
        keep.append(kept)
        recv.append(lax.ppermute(sent, "dp", CORE_PAIRS))

    cut = pair_sum(keep, recv)
    by_x, by_z = cut[:4], cut[4:]
    by_x = [by_x[0]] + [lax.ppermute(by_x[s], "dp", along_x(s)) for s in (1, 2, 3)]
    by_z = [by_z[0]] + [lax.ppermute(by_z[s], "dp", along_z(s)) for s in (1, 2, 3)]
    by_x = stage_sum(by_x)
    by_z = stage_sum(by_z)
    first = [by_x[0]] + [lax.ppermute(by_x[s], "dp", along_z(s)) for s in (1, 2, 3)]
    second = [by_z[0]] + [lax.ppermute(by_z[s], "dp", along_x(s)) for s in (1, 2, 3)]
    mine, fix, squares = owned_sum(first, second, devices)
    fix = lax.ppermute(fix, "dp", CORE_PAIRS)
    squares = lax.all_to_all(squares, ("dp", "tensor"), 0, 0, tiled=True)

    limit_sq = float(3 * bases.shape[2] * total_units)
    new_first, new_second, way = adam(
        limit_sq, place, squares, mine, fix, first_moment[:, 0], second_moment[:, 0]
    )
    pieces = lax.all_to_all(updates(way, bases), "dp", 0, 0, tiled=True)
    gate_update, up_update, down_update = layout(pieces)
    return (gate_update, up_update, down_update, new_first[:, None], new_second[:, None])


def solution(mesh):
    placed = (
        P("dp", None),
        P(None, "dp", "tensor"),
        P("dp", "tensor"),
        P("dp", None),
        P(),
        P(None, "tensor", "dp", None),
        P(None, "tensor", "dp", None),
    )
    return jax.shard_map(
        body,
        mesh=mesh,
        in_specs=placed,
        out_specs=(
            P("dp", "tensor"),
            P("dp", "tensor"),
            P("tensor", "dp"),
            P(None, "tensor", "dp", None),
            P(None, "tensor", "dp", None),
        ),
        check_vma=False,
    )
```

```python
import functools

import jax
import jax.numpy as jnp
from jax import lax
from jax.experimental import pallas as pl
from jax.experimental.pallas import tpu as pltpu
from jax.sharding import PartitionSpec as P

STEP = 10
N_Z, N_X, N_C = 4, 4, 2
N_DP = N_Z * N_X * N_C
UNITS = 86
PAD = 88
LANES = 128
BF16 = jnp.bfloat16
F32 = jnp.float32
MB = 1 << 20


def dp_index(z, x, c):
    return ((z % N_Z) * N_X + (x % N_X)) * N_C + c % N_C


def every_chip():
    return [(z, x, c) for z in range(N_Z) for x in range(N_X) for c in range(N_C)]


CORE_PAIRS = [(dp_index(z, x, c), dp_index(z, x, c + 1)) for z, x, c in every_chip()]


def along_x(s):
    return [(dp_index(z, x, c), dp_index(z, x + s, c)) for z, x, c in every_chip()]


def along_z(s):
    return [(dp_index(z, x, c), dp_index(z + s, x, c)) for z, x, c in every_chip()]


VMEM = pl.BlockSpec(memory_space=pltpu.VMEM)
SMEM = pl.BlockSpec(memory_space=pltpu.SMEM)


def params(mib, **more):
    return pltpu.CompilerParams(vmem_limit_bytes=mib * MB, **more)


def project_kernel(b_steps, a_ref, b_ref, g_ref, send_ref, kept_ref, acc, other, terms):
    k = pl.program_id(0)
    count = b_ref.shape[0]
    half = kept_ref.shape[2]

    @pl.when(k < b_steps)
    def _():
        for m in range(count):
            part = jnp.dot(a_ref[...], b_ref[m], preferred_element_type=F32)

            @pl.when(k == 0)
            def _(m=m, part=part):
                acc[m] = part

            @pl.when(k > 0)
            def _(m=m, part=part):
                acc[m] += part

    @pl.when(k == b_steps)
    def _():
        terms[...] = jnp.zeros(terms.shape, F32)
        core = lax.rem(lax.axis_index("dp"), 2)
        for m in range(count):
            low, high = acc[m, :, :half].astype(BF16), acc[m, :, half:].astype(BF16)
            kept_ref[m] = jnp.where(core == 0, low, high)
            other[m] = jnp.where(core == 0, high, low)

    @pl.when(k >= b_steps)
    def _():
        block = g_ref.shape[1]
        for m in range(count):
            terms[m, :block] = jnp.dot(g_ref[m], other[m], preferred_element_type=F32)
            for d in range(block // UNITS):
                send_ref[m, 0, d] = terms[m, d * UNITS : d * UNITS + PAD].astype(BF16)


def project(a, bases, first, g):
    tokens, width = a.shape
    rank = bases.shape[2]
    count, units, _ = g.shape
    half = rank // 2
    steps = 8
    wide = width // steps
    block = units // N_Z
    chunks = block // UNITS
    last = lambda k: jnp.minimum(k, steps - 1)
    after = lambda k: jnp.maximum(k - steps, 0)
    return pl.pallas_call(
        functools.partial(project_kernel, steps),
        grid=(steps + N_Z,),
        in_specs=[
            pl.BlockSpec((tokens, wide), lambda k: (0, last(k))),
            pl.BlockSpec((count, wide, rank), lambda k: (first // count, last(k), 0)),
            pl.BlockSpec((count, block, tokens), lambda k: (0, after(k), 0)),
        ],
        out_specs=[
            pl.BlockSpec((count, 1, chunks, PAD, half), lambda k: (0, after(k), 0, 0, 0)),
            pl.BlockSpec((count, tokens, half), lambda k: (0, 0, 0)),
        ],
        out_shape=[
            jax.ShapeDtypeStruct((count, N_Z, chunks, PAD, half), BF16),
            jax.ShapeDtypeStruct((count, tokens, half), BF16),
        ],
        scratch_shapes=[
            pltpu.VMEM((count, tokens, rank), F32),
            pltpu.VMEM((count, tokens, half), BF16),
            pltpu.VMEM((count, block + 8, half), F32),
        ],
        compiler_params=params(56),
        cost_estimate=pl.CostEstimate(
            flops=2 * count * tokens * rank * (width + units // 2),
            bytes_accessed=2 * (tokens * width + count * (width * rank + tokens * units + units * half)),
            transcendentals=0,
        ),
        name="project",
    )(a, bases, g)


def collect_kernel(old, place, g_ref, kept_ref, recv_ref, *refs):
    by_x, by_z = refs[old : old + 4], refs[old + 4 : old + 8]
    terms, cut = refs[old + 8 :]
    step = pl.program_id(0)
    x0, c0 = place[1], place[2]
    count, block, _ = g_ref.shape

    @pl.when(step == 0)
    def _():
        terms[...] = jnp.zeros(terms.shape, F32)

    for m in range(count):
        terms[m, :block] = jnp.dot(g_ref[m], kept_ref[m], preferred_element_type=F32)
        for x in range(N_X):
            sx = lax.rem(x - x0 + N_X, N_X)
            for c in range(N_C):
                own = lax.rem(c + c0, 2)
                d = x * N_C + c
                both = terms[m, d * UNITS : d * UNITS + PAD] + recv_ref[m, 0, d].astype(F32)
                both = both.astype(BF16)
                cut[0, sx, m, own] = both[:, :LANES]
                cut[1, sx, m, own] = both[:, LANES:]
    for s in range(N_X):
        by_x[s][0] = cut[0, s]
    for s in range(N_Z):

        @pl.when(step == s)
        def _(s=s):
            by_z[s][...] = cut[1]


def collect(place, g, kept, recv, first, old=()):
    count, units, tokens = g.shape
    half = kept.shape[2]
    block = units // N_Z
    chunks = block // UNITS
    shape = (4, 3, N_C, PAD, LANES)
    at = first // count
    ring = lambda i, s: lax.rem(s[0] + i, N_Z)
    return pl.pallas_call(
        functools.partial(collect_kernel, len(old)),
        grid_spec=pltpu.PrefetchScalarGridSpec(
            num_scalar_prefetch=1,
            grid=(N_Z,),
            in_specs=[
                pl.BlockSpec((count, block, tokens), lambda i, s: (0, ring(i, s), 0)),
                pl.BlockSpec((count, tokens, half), lambda i, s: (0, 0, 0)),
                pl.BlockSpec((count, 1, chunks, PAD, half), lambda i, s: (0, ring(i, s), 0, 0, 0)),
            ]
            + [pl.BlockSpec(memory_space=pl.ANY)] * len(old),
            out_specs=[pl.BlockSpec((1, count, N_C, PAD, LANES), lambda i, s: (i, at, 0, 0, 0))] * 4
            + [pl.BlockSpec((4, count, N_C, PAD, LANES), lambda i, s: (0, at, 0, 0, 0))] * 4,
            scratch_shapes=[
                pltpu.VMEM((count, block + 8, half), F32),
                pltpu.VMEM((2, 4, count, N_C, PAD, LANES), BF16),
            ],
        ),
        out_shape=[jax.ShapeDtypeStruct(shape, BF16)] * 8,
        input_output_aliases={4 + i: i for i in range(len(old))},
        compiler_params=params(32),
        cost_estimate=pl.CostEstimate(
            flops=2 * count * tokens * units * half,
            bytes_accessed=2 * count * units * (tokens + 2 * half),
            transcendentals=0,
        ),
        name="collect",
    )(place, g, kept, recv, *old)


def stage_kernel(own, r1, r2, r3, *outs):
    for i, out in enumerate(outs):
        total = own[i].astype(F32) + r1[i].astype(F32)
        total = total + (r2[i].astype(F32) + r3[i].astype(F32))
        out[...] = total.astype(BF16)


def stage_sum(terms):
    shape = terms[0].shape[1:]
    return pl.pallas_call(
        stage_kernel,
        in_specs=[VMEM] * 4,
        out_specs=[VMEM] * 4,
        out_shape=[jax.ShapeDtypeStruct(shape, BF16)] * 4,
        compiler_params=params(16),
        name="stage_sum",
    )(*terms)


def owned_kernel(*refs):
    parts, (mine, fix, squares) = refs[:8], refs[8:]
    inside = lax.broadcasted_iota(jnp.int32, (PAD, LANES), 0) < UNITS
    total_sq = jnp.zeros((PAD, LANES), F32)
    for half in range(2):
        t = parts[4 * half : 4 * half + 4]
        lanes = slice(half * LANES, half * LANES + LANES)
        for m in range(3):
            for c in range(N_C):
                v = t[0][m, c].astype(F32) + t[1][m, c].astype(F32)
                v = v + (t[2][m, c].astype(F32) + t[3][m, c].astype(F32))
                total_sq += jnp.where(inside, v * v, 0.0)
                if c == 0:
                    mine[m, :, lanes] = v
                else:
                    fix[m, :, lanes] = v.astype(BF16)
    row = jnp.sum(total_sq, axis=0, keepdims=True)
    squares[...] = jnp.broadcast_to(row, squares.shape)


def owned_sum(first, second, peers):
    return pl.pallas_call(
        owned_kernel,
        in_specs=[VMEM] * 8,
        out_specs=[VMEM] * 3,
        out_shape=[
            jax.ShapeDtypeStruct((3, PAD, 2 * LANES), F32),
            jax.ShapeDtypeStruct((3, PAD, 2 * LANES), BF16),
            jax.ShapeDtypeStruct((peers, LANES), F32),
        ],
        compiler_params=params(16),
        name="owned_sum",
    )(*first, *second)


def adam_kernel(limit_sq, place, squares, mine, recv, first, second, new_first, new_second, direction):
    total = jnp.sum(squares[...])
    clip_limit = jnp.sqrt(jnp.full((1, 1), limit_sq, F32))
    factor = jnp.minimum(1.0, clip_limit / jnp.sqrt(jnp.full((1, 1), total, F32)))
    low = place[2] == 0
    for m in range(3):
        here = mine[m]
        there = recv[m].astype(F32)
        lower = jnp.where(low, here, there)
        upper = jnp.where(low, there, here)
        clipped = jnp.concatenate([lower, upper], axis=1)[:UNITS] * factor
        one = 0.9 * first[m] + 0.1 * clipped
        two = 0.95 * second[m] + 0.05 * clipped * clipped
        new_first[m] = one
        new_second[m] = two
        way = one / (1.0 - 0.9**STEP) / (jnp.sqrt(two / (1.0 - 0.95**STEP)) + 1e-08)
        padded = jnp.concatenate([way, jnp.zeros((PAD - UNITS, way.shape[1]), F32)], axis=0)
        direction[m] = padded.astype(BF16)


def adam(limit_sq, place, squares, mine, recv, first, second):
    rank = first.shape[-1]
    moment = jax.ShapeDtypeStruct((3, UNITS, rank), F32)
    return pl.pallas_call(
        functools.partial(adam_kernel, limit_sq),
        in_specs=[SMEM] + [VMEM] * 5,
        out_specs=[VMEM] * 3,
        out_shape=[moment, moment, jax.ShapeDtypeStruct((3, PAD, rank), BF16)],
        compiler_params=params(16),
        name="adam",
    )(place, squares, mine, recv, first, second)


def update_kernel(way, bases, out):
    for m in range(3):
        full = lax.dot_general(
            way[m], bases[m], (((1,), (1,)), ((), ())), preferred_element_type=F32
        ).astype(BF16)
        for j in range(out.shape[0]):
            out[j, m] = full[:, j * LANES : (j + 1) * LANES]


def updates(way, bases):
    width, rank = bases.shape[1:]
    wide = 512
    shape = (width // LANES, 3, PAD, LANES)
    return pl.pallas_call(
        update_kernel,
        grid=(width // wide,),
        in_specs=[
            pl.BlockSpec((3, PAD, rank), lambda i: (0, 0, 0)),
            pl.BlockSpec((3, wide, rank), lambda i: (0, i, 0)),
        ],
        out_specs=pl.BlockSpec((wide // LANES, 3, PAD, LANES), lambda i: (i, 0, 0, 0)),
        out_shape=jax.ShapeDtypeStruct(shape, BF16),
        compiler_params=params(56),
        name="updates",
    )(way, bases)


def layout_kernel(pieces, gate, up, down, rows):
    units = N_DP * UNITS
    for m, out in enumerate((gate, up, down)):
        for k in range(N_DP):
            rows[m, k * UNITS : k * UNITS + PAD, :] = pieces[k, m].astype(F32)
        out[...] = rows[m, :units, :].astype(BF16)


def layout(pieces):
    units = N_DP * UNITS
    return pl.pallas_call(
        layout_kernel,
        in_specs=[VMEM],
        out_specs=[VMEM] * 3,
        out_shape=[jax.ShapeDtypeStruct((units, LANES), BF16)] * 3,
        scratch_shapes=[pltpu.VMEM((3, units + 8, LANES), F32)],
        compiler_params=params(24),
        name="layout",
    )(pieces)


def body(activations, gate_up_grads, hidden_act, down_out_grad, bases, first_moment, second_moment):
    devices = lax.axis_size("dp") * lax.axis_size("tensor")
    total_units = hidden_act.shape[1] * lax.axis_size("tensor")
    me = lax.axis_index("dp")
    place = jnp.stack([me // (N_X * N_C), (me // N_C) % N_X, me % N_C]).astype(jnp.int32)

    gate_up = jnp.swapaxes(gate_up_grads, 1, 2)
    hidden = hidden_act.T[None]
    sent_two, kept_two = project(activations, bases, 0, gate_up)
    recv_two = lax.ppermute(sent_two, "dp", CORE_PAIRS)
    sent_one, kept_one = project(down_out_grad, bases, 2, hidden)
    recv_one = lax.ppermute(sent_one, "dp", CORE_PAIRS)
    cut = collect(place, gate_up, kept_two, recv_two, 0)
    cut = collect(place, hidden, kept_one, recv_one, 2, cut)
    by_x, by_z = cut[:4], cut[4:]
    by_x = [by_x[0]] + [lax.ppermute(by_x[s], "dp", along_x(s)) for s in (1, 2, 3)]
    by_z = [by_z[0]] + [lax.ppermute(by_z[s], "dp", along_z(s)) for s in (1, 2, 3)]
    by_x = stage_sum(by_x)
    by_z = stage_sum(by_z)
    first = [by_x[0]] + [lax.ppermute(by_x[s], "dp", along_z(s)) for s in (1, 2, 3)]
    second = [by_z[0]] + [lax.ppermute(by_z[s], "dp", along_x(s)) for s in (1, 2, 3)]
    mine, fix, squares = owned_sum(first, second, devices)
    fix = lax.ppermute(fix, "dp", CORE_PAIRS)
    squares = lax.all_to_all(squares, ("dp", "tensor"), 0, 0, tiled=True)

    limit_sq = float(3 * bases.shape[2] * total_units)
    new_first, new_second, way = adam(
        limit_sq, place, squares, mine, fix, first_moment[:, 0], second_moment[:, 0]
    )
    pieces = lax.all_to_all(updates(way, bases), "dp", 0, 0, tiled=True)
    gate_update, up_update, down_update = layout(pieces)
    return (gate_update.T, up_update.T, down_update, new_first[:, None], new_second[:, None])


def solution(mesh):
    placed = (
        P("dp", None),
        P(None, "dp", "tensor"),
        P("dp", "tensor"),
        P("dp", None),
        P(),
        P(None, "tensor", "dp", None),
        P(None, "tensor", "dp", None),
    )
    return jax.shard_map(
        body,
        mesh=mesh,
        in_specs=placed,
        out_specs=(
            P("dp", "tensor"),
            P("dp", "tensor"),
            P("tensor", "dp"),
            P(None, "tensor", "dp", None),
            P(None, "tensor", "dp", None),
        ),
        check_vma=False,
    )
```

```python
import functools

import jax
import jax.numpy as jnp
from jax import lax
from jax.experimental import pallas as pl
from jax.experimental.pallas import tpu as pltpu
from jax.sharding import PartitionSpec as P

STEP = 10
N_Z, N_X, N_C = 4, 4, 2
N_DP = N_Z * N_X * N_C
UNITS = 86
PAD = 88
LANES = 128
BF16 = jnp.bfloat16
F32 = jnp.float32
MB = 1 << 20


def dp_index(z, x, c):
    return ((z % N_Z) * N_X + (x % N_X)) * N_C + c % N_C


def every_chip():
    return [(z, x, c) for z in range(N_Z) for x in range(N_X) for c in range(N_C)]


CORE_PAIRS = [(dp_index(z, x, c), dp_index(z, x, c + 1)) for z, x, c in every_chip()]


FLIPS = ((1, 3), (3, 1))
FLIP_ORDER = tuple((0, b, a, a ^ b) for a, b in FLIPS)
RANK_OF = tuple(tuple(order.index(d) for d in range(4)) for order in FLIP_ORDER)


def along_x(turn):
    return [(dp_index(z, x, c), dp_index(z, x ^ FLIPS[c][turn], c)) for z, x, c in every_chip()]


def along_z(turn):
    return [(dp_index(z, x, c), dp_index(z ^ FLIPS[c][turn], x, c)) for z, x, c in every_chip()]


VMEM = pl.BlockSpec(memory_space=pltpu.VMEM)
SMEM = pl.BlockSpec(memory_space=pltpu.SMEM)
ANY = pl.BlockSpec(memory_space=pl.ANY)


def params(mib, **more):
    return pltpu.CompilerParams(vmem_limit_bytes=mib * MB, **more)


def project_kernel(steps, window, place, x_hbm, y_hbm, b_hbm, kept, sent, x, y, b, acc, sem_a, sem_b):
    wide = x.shape[1] // steps
    half = kept.shape[2]
    jobs = [(x_hbm, x, 0, (0, 1), k) for k in range(steps)] + [
        (y_hbm, y, 1, (2,), k) for k in range(steps)
    ]

    def copies(job):
        src, dst, which, matrices, k = job
        at = pl.ds(k * wide, wide)
        yield pltpu.make_async_copy(src.at[:, at], dst.at[:, at], sem_a.at[which, k])
        for m in matrices:
            yield pltpu.make_async_copy(b_hbm.at[m, at], b.at[m, at], sem_b.at[m, k])

    for job in jobs[:window]:
        for copy in copies(job):
            copy.start()
    for i, job in enumerate(jobs):
        for copy in copies(job):
            copy.wait()
        if i + window < len(jobs):
            for copy in copies(jobs[i + window]):
                copy.start()
        _, rows, _, matrices, k = job
        at = slice(k * wide, (k + 1) * wide)
        for m in matrices:
            part = jnp.dot(rows[:, at], b[m, at], preferred_element_type=F32)
            if k == 0:
                acc[m] = part
            elif k < steps - 1:
                acc[m] += part
            else:
                full = (acc[m] + part).astype(BF16)
                low, high = full[:, :half], full[:, half:]
                first = place[8] == 0
                kept[m] = jnp.where(first, low, high)
                sent[m] = jnp.where(first, high, low)


def project(place, x, y, bases):
    tokens, width = x.shape
    rank = bases.shape[2]
    steps = 8
    out = jax.ShapeDtypeStruct((3, tokens, rank // 2), BF16)
    return pl.pallas_call(
        functools.partial(project_kernel, steps, 4),
        in_specs=[SMEM, ANY, ANY, ANY],
        out_specs=[VMEM] * 2,
        out_shape=[out, out],
        scratch_shapes=[
            pltpu.VMEM((tokens, width), BF16),
            pltpu.VMEM((tokens, width), BF16),
            pltpu.VMEM((3, width, rank), BF16),
            pltpu.VMEM((3, tokens, rank), F32),
            pltpu.SemaphoreType.DMA((2, steps)),
            pltpu.SemaphoreType.DMA((3, steps)),
        ],
        compiler_params=params(58),
        cost_estimate=pl.CostEstimate(
            flops=2 * 3 * tokens * rank * width,
            bytes_accessed=2 * (2 * tokens * width + 3 * width * rank),
            transcendentals=0,
        ),
        name="project",
    )(place, x, y, bases)


def collect_kernel(place, g_two, g_one, h_two, h_one, mine, theirs, xa, xb, za, zb, terms, cut):
    step = pl.program_id(0)
    c0 = place[8]
    block = g_two.shape[1]

    @pl.when(step == 0)
    def _():
        terms[...] = jnp.zeros(terms.shape, F32)

    for m in range(3):
        here = g_two[m] if m < 2 else g_one[0]
        there = h_two[m] if m < 2 else h_one[0]
        terms[m, :block] = jnp.dot(here, mine[m], preferred_element_type=F32) + jnp.dot(
            there, theirs[m], preferred_element_type=F32
        )
        for x in range(N_X):
            at = place[4 + x]
            for c in range(N_C):
                own = lax.rem(c + c0, 2)
                d = (x * N_C + c) * UNITS
                both = terms[m, d : d + PAD].astype(BF16)
                cut[0, at, m, own] = both[:, :LANES]
                cut[1, at, m, own] = both[:, LANES:]
    xa[:, 0] = cut[0, :2]
    xb[:, 0] = cut[0, 2:]

    @pl.when(step < 2)
    def _():
        za[0] = cut[1]

    @pl.when(step >= 2)
    def _():
        zb[0] = cut[1]


def collect(place, g_two, g_one, h_two, h_one, mine, theirs):
    _, units, tokens = g_two.shape
    half = mine.shape[2]
    block = units // N_Z
    shape = (2, 4, 3, N_C, PAD, LANES)
    by_z = lambda count: pl.BlockSpec((count, block, tokens), lambda i, s: (0, s[i], 0))
    whole = pl.BlockSpec((3, tokens, half), lambda i, s: (0, 0, 0))
    x_spec = pl.BlockSpec((2, 1, 3, N_C, PAD, LANES), lambda i, s: (0, i, 0, 0, 0, 0))
    z_shape = (1, 4, 3, N_C, PAD, LANES)
    return pl.pallas_call(
        collect_kernel,
        grid_spec=pltpu.PrefetchScalarGridSpec(
            num_scalar_prefetch=1,
            grid=(N_Z,),
            in_specs=[by_z(2), by_z(1), by_z(2), by_z(1), whole, whole],
            out_specs=[
                x_spec,
                x_spec,
                pl.BlockSpec(z_shape, lambda i, s: (jnp.minimum(i, 1), 0, 0, 0, 0, 0)),
                pl.BlockSpec(z_shape, lambda i, s: (jnp.maximum(i - 2, 0), 0, 0, 0, 0, 0)),
            ],
            scratch_shapes=[
                pltpu.VMEM((3, block + 8, half), F32),
                pltpu.VMEM((2, 4, 3, N_C, PAD, LANES), BF16),
            ],
        ),
        out_shape=[jax.ShapeDtypeStruct(shape, BF16)] * 4,
        compiler_params=params(58),
        cost_estimate=pl.CostEstimate(
            flops=2 * 3 * 2 * tokens * units * half,
            bytes_accessed=2 * 3 * units * (2 * tokens + half),
            transcendentals=0,
        ),
        name="collect",
    )(place, g_two, g_one, h_two, h_one, mine, theirs)


def halve_kernel(kept, recv, stay, go):
    n = kept.shape[0] // 2
    for out, at in ((stay, slice(0, n)), (go, slice(n, 2 * n))):
        out[...] = (kept[at].astype(F32) + recv[at].astype(F32)).astype(BF16)


def halve(kept, recv):
    shape = (kept.shape[0] // 2, *kept.shape[1:])
    return pl.pallas_call(
        halve_kernel,
        in_specs=[VMEM] * 2,
        out_specs=[VMEM] * 2,
        out_shape=[jax.ShapeDtypeStruct(shape, BF16)] * 2,
        compiler_params=params(12),
        name="halve",
    )(kept, recv)


def owned_kernel(xa, xb, za, zb, mine, fix, squares):
    inside = lax.broadcasted_iota(jnp.int32, (PAD, LANES), 0) < UNITS
    total_sq = jnp.zeros((PAD, LANES), F32)
    for half, (p, q) in enumerate(((xa, xb), (za, zb))):
        lanes = slice(half * LANES, half * LANES + LANES)
        for m in range(3):
            for c in range(N_C):
                v = p[0, m, c].astype(F32) + q[0, m, c].astype(F32)
                total_sq += jnp.where(inside, v * v, 0.0)
                if c == 0:
                    mine[m, :, lanes] = v
                else:
                    fix[m, :, lanes] = v.astype(BF16)
    row = jnp.sum(total_sq, axis=0, keepdims=True)
    squares[...] = jnp.broadcast_to(row, squares.shape)


def owned_sum(xa, xb, za, zb, peers):
    return pl.pallas_call(
        owned_kernel,
        in_specs=[VMEM] * 4,
        out_specs=[VMEM] * 3,
        out_shape=[
            jax.ShapeDtypeStruct((3, PAD, 2 * LANES), F32),
            jax.ShapeDtypeStruct((3, PAD, 2 * LANES), BF16),
            jax.ShapeDtypeStruct((peers, LANES), F32),
        ],
        compiler_params=params(12),
        name="owned_sum",
    )(xa, xb, za, zb)


def update_kernel(
    limit_sq, window, place, squares, mine, recv, first, second, b_hbm, new_first, new_second, out, b, way, sem
):
    pieces = sem.shape[1]
    wide = b.shape[1] // pieces
    jobs = [(j, m) for j in range(pieces) for m in range(3)]

    def copy(job):
        j, m = job
        at = pl.ds(j * wide, wide)
        return pltpu.make_async_copy(b_hbm.at[m, at], b.at[m, at], sem.at[m, j])

    for job in jobs[:window]:
        copy(job).start()

    total = jnp.sum(squares[...])
    clip_limit = jnp.sqrt(jnp.full((1, 1), limit_sq, F32))
    factor = jnp.minimum(1.0, clip_limit / jnp.sqrt(jnp.full((1, 1), total, F32)))
    low = place[8] == 0
    for m in range(3):
        here = mine[m]
        there = recv[m].astype(F32)
        lower = jnp.where(low, here, there)
        upper = jnp.where(low, there, here)
        clipped = jnp.concatenate([lower, upper], axis=1)[:UNITS] * factor
        one = 0.9 * first[m] + 0.1 * clipped
        two = 0.95 * second[m] + 0.05 * clipped * clipped
        new_first[m] = one
        new_second[m] = two
        turn = one / (1.0 - 0.9**STEP) / (jnp.sqrt(two / (1.0 - 0.95**STEP)) + 1e-08)
        rows = way.shape[1] - UNITS
        padded = jnp.concatenate([turn, jnp.zeros((rows, turn.shape[1]), F32)], axis=0)
        way[m] = padded.astype(BF16)

    for i, (j, m) in enumerate(jobs):
        copy((j, m)).wait()
        if i + window < len(jobs):
            copy(jobs[i + window]).start()
        full = lax.dot_general(
            way[m], b[m, j * wide : (j + 1) * wide], (((1,), (1,)), ((), ())), preferred_element_type=F32
        ).astype(BF16)
        for n in range(wide // LANES):
            out[j * (wide // LANES) + n, m] = full[:, n * LANES : (n + 1) * LANES]


def update(limit_sq, place, squares, mine, recv, first, second, bases):
    _, width, rank = bases.shape
    moment = jax.ShapeDtypeStruct((3, UNITS, rank), F32)
    return pl.pallas_call(
        functools.partial(update_kernel, limit_sq, 8),
        in_specs=[SMEM] + [VMEM] * 5 + [ANY],
        out_specs=[VMEM] * 3,
        out_shape=[
            moment,
            moment,
            jax.ShapeDtypeStruct((width // LANES, 3, PAD, LANES), BF16),
        ],
        scratch_shapes=[
            pltpu.VMEM((3, width, rank), BF16),
            pltpu.VMEM((3, PAD, rank), BF16),
            pltpu.SemaphoreType.DMA((3, 8)),
        ],
        compiler_params=params(48),
        name="update",
    )(place, squares, mine, recv, first, second, bases)


def layout_kernel(pieces, gate, up, down, rows):
    units = N_DP * UNITS
    for m, out in enumerate((gate, up, down)):
        for k in range(N_DP):
            rows[m, k * UNITS : k * UNITS + PAD, :] = pieces[k, m].astype(F32)
        out[...] = rows[m, :units, :].astype(BF16)


def layout(pieces):
    units = N_DP * UNITS
    return pl.pallas_call(
        layout_kernel,
        in_specs=[VMEM],
        out_specs=[VMEM] * 3,
        out_shape=[jax.ShapeDtypeStruct((units, LANES), BF16)] * 3,
        scratch_shapes=[pltpu.VMEM((3, units + 8, LANES), F32)],
        compiler_params=params(24),
        name="layout",
    )(pieces)


def body(activations, gate_up_grads, hidden_act, down_out_grad, bases, first_moment, second_moment):
    devices = lax.axis_size("dp") * lax.axis_size("tensor")
    total_units = hidden_act.shape[1] * lax.axis_size("tensor")
    me = lax.axis_index("dp")
    z, x, c = me // (N_X * N_C), (me // N_C) % N_X, me % N_C
    order = jnp.asarray(FLIP_ORDER, jnp.int32)[c]
    ranks = jnp.asarray(RANK_OF, jnp.int32)[c]
    across = ranks[jnp.bitwise_xor(jnp.arange(N_X, dtype=jnp.int32), x)]
    place = jnp.concatenate([jnp.bitwise_xor(order, z), across, c[None]]).astype(jnp.int32)

    gate_up = jnp.swapaxes(gate_up_grads, 1, 2)
    hidden = hidden_act.T[None]
    gate_up_there = lax.ppermute(gate_up, "dp", CORE_PAIRS)
    hidden_there = lax.ppermute(hidden, "dp", CORE_PAIRS)
    kept, sent = project(place, activations, down_out_grad, bases)
    theirs = lax.ppermute(sent, "dp", CORE_PAIRS)
    xa, xb, za, zb = collect(place, gate_up, hidden, gate_up_there, hidden_there, kept, theirs)

    rounds = [(along_x, along_z, 0), (along_x, along_z, 1), (along_z, along_x, 0), (along_z, along_x, 1)]
    for i, (one_way, other_way, turn) in enumerate(rounds):
        xr = lax.ppermute(xb, "dp", one_way(turn))
        zr = lax.ppermute(zb, "dp", other_way(turn))
        if i == 1:
            xa, xr, za, zr = xa[0], xr[0], za[0], zr[0]
        if i < 3:
            xa, xb = halve(xa, xr)
            za, zb = halve(za, zr)

    mine, fix, squares = owned_sum(xa, xr, za, zr, devices)
    fix = lax.ppermute(fix, "dp", CORE_PAIRS)
    squares = lax.all_to_all(squares, ("dp", "tensor"), 0, 0, tiled=True)

    limit_sq = float(3 * bases.shape[2] * total_units)
    new_first, new_second, pieces = update(
        limit_sq, place, squares, mine, fix, first_moment[:, 0], second_moment[:, 0], bases
    )
    pieces = lax.all_to_all(pieces, "dp", 0, 0, tiled=True)
    gate_update, up_update, down_update = layout(pieces)
    return (gate_update.T, up_update.T, down_update, new_first[:, None], new_second[:, None])


def solution(mesh):
    placed = (
        P("dp", None),
        P(None, "dp", "tensor"),
        P("dp", "tensor"),
        P("dp", None),
        P(),
        P(None, "tensor", "dp", None),
        P(None, "tensor", "dp", None),
    )
    return jax.shard_map(
        body,
        mesh=mesh,
        in_specs=placed,
        out_specs=(
            P("dp", "tensor"),
            P("dp", "tensor"),
            P("tensor", "dp"),
            P(None, "tensor", "dp", None),
            P(None, "tensor", "dp", None),
        ),
        check_vma=False,
    )
```

```python
import functools

import jax
import jax.numpy as jnp
import numpy as np
from jax import lax
from jax.experimental import pallas as pl
from jax.experimental.pallas import tpu as pltpu
from jax.sharding import PartitionSpec as P

STEP = 10
N_Z, N_X, N_C = 4, 4, 2
N_DP = N_Z * N_X * N_C
UNITS = 86
PAD = 88
LANES = 128
BF16 = jnp.bfloat16
F32 = jnp.float32
MB = 1 << 20


def dp_index(z, x, c):
    return ((z % N_Z) * N_X + (x % N_X)) * N_C + c % N_C


def every_chip():
    return [(z, x, c) for z in range(N_Z) for x in range(N_X) for c in range(N_C)]


CORE_PAIRS = [(dp_index(z, x, c), dp_index(z, x, c + 1)) for z, x, c in every_chip()]


FLIPS = ((1, 3), (3, 1))
FLIP_ORDER = tuple((0, b, a, a ^ b) for a, b in FLIPS)
RANK_OF = tuple(tuple(order.index(d) for d in range(4)) for order in FLIP_ORDER)


def along_x(turn):
    return [(dp_index(z, x, c), dp_index(z, x ^ FLIPS[c][turn], c)) for z, x, c in every_chip()]


def along_z(turn):
    return [(dp_index(z, x, c), dp_index(z ^ FLIPS[c][turn], x, c)) for z, x, c in every_chip()]


def direct_x(r):
    return [(dp_index(z, x, c), dp_index(z, x ^ FLIP_ORDER[c][r], c)) for z, x, c in every_chip()]


def direct_z(r):
    return [(dp_index(z, x, c), dp_index(z ^ FLIP_ORDER[c][r], x, c)) for z, x, c in every_chip()]


PLACES = np.array(
    [
        [z ^ d for d in FLIP_ORDER[c]] + [RANK_OF[c][block ^ x] for block in range(N_X)] + [c]
        for z, x, c in every_chip()
    ],
    np.int32,
)


VMEM = pl.BlockSpec(memory_space=pltpu.VMEM)
SMEM = pl.BlockSpec(memory_space=pltpu.SMEM)
ANY = pl.BlockSpec(memory_space=pl.ANY)


def params(mib, **more):
    return pltpu.CompilerParams(vmem_limit_bytes=mib * MB, **more)


def project_kernel(steps, window, place, x_hbm, y_hbm, b_hbm, kept, sent, x, y, b, acc, sem_a, sem_b):
    wide = x.shape[1] // steps
    half = kept.shape[2]
    jobs = [(x_hbm, x, 0, (0, 1), k) for k in range(steps)] + [
        (y_hbm, y, 1, (2,), k) for k in range(steps)
    ]

    def copies(job):
        src, dst, which, matrices, k = job
        at = pl.ds(k * wide, wide)
        yield pltpu.make_async_copy(src.at[:, at], dst.at[:, at], sem_a.at[which, k])
        for m in matrices:
            yield pltpu.make_async_copy(b_hbm.at[m, at], b.at[m, at], sem_b.at[m, k])

    for job in jobs[:window]:
        for copy in copies(job):
            copy.start()
    for i, job in enumerate(jobs):
        for copy in copies(job):
            copy.wait()
        if i + window < len(jobs):
            for copy in copies(jobs[i + window]):
                copy.start()
        _, rows, _, matrices, k = job
        at = slice(k * wide, (k + 1) * wide)
        for m in matrices:
            part = jnp.dot(rows[:, at], b[m, at], preferred_element_type=F32)
            if k == 0:
                acc[m] = part
            elif k < steps - 1:
                acc[m] += part
            else:
                full = (acc[m] + part).astype(BF16)
                low, high = full[:, :half], full[:, half:]
                first = place[8] == 0
                kept[m] = jnp.where(first, low, high)
                sent[m] = jnp.where(first, high, low)


def project(place, x, y, bases):
    tokens, width = x.shape
    rank = bases.shape[2]
    steps = 8
    out = jax.ShapeDtypeStruct((3, tokens, rank // 2), BF16)
    return pl.pallas_call(
        functools.partial(project_kernel, steps, 4),
        in_specs=[SMEM, ANY, ANY, ANY],
        out_specs=[VMEM] * 2,
        out_shape=[out, out],
        scratch_shapes=[
            pltpu.VMEM((tokens, width), BF16),
            pltpu.VMEM((tokens, width), BF16),
            pltpu.VMEM((3, width, rank), BF16),
            pltpu.VMEM((3, tokens, rank), F32),
            pltpu.SemaphoreType.DMA((2, steps)),
            pltpu.SemaphoreType.DMA((3, steps)),
        ],
        compiler_params=params(58),
        cost_estimate=pl.CostEstimate(
            flops=2 * 3 * tokens * rank * width,
            bytes_accessed=2 * (2 * tokens * width + 3 * width * rank),
            transcendentals=0,
        ),
        name="project",
    )(place, x, y, bases)


def collect_kernel(place, g_two, g_one, h_two, h_one, mine, theirs, xa, xb, za, zb, terms, cut):
    step = pl.program_id(0)
    c0 = place[8]
    block = g_two.shape[1]

    @pl.when(step == 0)
    def _():
        terms[...] = jnp.zeros(terms.shape, F32)

    for m in range(3):
        here = g_two[m] if m < 2 else g_one[0]
        there = h_two[m] if m < 2 else h_one[0]
        terms[m, :block] = jnp.dot(here, mine[m], preferred_element_type=F32) + jnp.dot(
            there, theirs[m], preferred_element_type=F32
        )
        for x in range(N_X):
            at = place[4 + x]
            for c in range(N_C):
                own = lax.rem(c + c0, 2)
                d = (x * N_C + c) * UNITS
                both = terms[m, d : d + PAD].astype(BF16)
                cut[0, at, m, own] = both[:, :LANES]
                cut[1, at, m, own] = both[:, LANES:]
    xa[:, 0] = cut[0, :2]
    xb[:, 0] = cut[0, 2:]

    @pl.when(step < 2)
    def _():
        za[0] = cut[1]

    @pl.when(step >= 2)
    def _():
        zb[0] = cut[1]


def collect(place, g_two, g_one, h_two, h_one, mine, theirs):
    _, units, tokens = g_two.shape
    half = mine.shape[2]
    block = units // N_Z
    shape = (2, 4, 3, N_C, PAD, LANES)
    by_z = lambda count: pl.BlockSpec((count, block, tokens), lambda i, s: (0, s[i], 0))
    whole = pl.BlockSpec((3, tokens, half), lambda i, s: (0, 0, 0))
    x_spec = pl.BlockSpec((2, 1, 3, N_C, PAD, LANES), lambda i, s: (0, i, 0, 0, 0, 0))
    z_shape = (1, 4, 3, N_C, PAD, LANES)
    return pl.pallas_call(
        collect_kernel,
        grid_spec=pltpu.PrefetchScalarGridSpec(
            num_scalar_prefetch=1,
            grid=(N_Z,),
            in_specs=[by_z(2), by_z(1), by_z(2), by_z(1), whole, whole],
            out_specs=[
                x_spec,
                x_spec,
                pl.BlockSpec(z_shape, lambda i, s: (jnp.minimum(i, 1), 0, 0, 0, 0, 0)),
                pl.BlockSpec(z_shape, lambda i, s: (jnp.maximum(i - 2, 0), 0, 0, 0, 0, 0)),
            ],
            scratch_shapes=[
                pltpu.VMEM((3, block + 8, half), F32),
                pltpu.VMEM((2, 4, 3, N_C, PAD, LANES), BF16),
            ],
        ),
        out_shape=[jax.ShapeDtypeStruct(shape, BF16)] * 4,
        compiler_params=params(24),
        cost_estimate=pl.CostEstimate(
            flops=2 * 3 * 2 * tokens * units * half,
            bytes_accessed=2 * 3 * units * (2 * tokens + half),
            transcendentals=0,
        ),
        name="collect",
    )(place, g_two, g_one, h_two, h_one, mine, theirs)


def split_kernel(kept, recv, *outs):
    n = kept.shape[0] // len(outs)
    for i, out in enumerate(outs):
        at = slice(i * n, (i + 1) * n)
        out[...] = (kept[at].astype(F32) + recv[at].astype(F32)).astype(BF16)


def split_sum(kept, recv, parts):
    shape = (kept.shape[0] // parts, *kept.shape[1:])
    return pl.pallas_call(
        split_kernel,
        in_specs=[VMEM] * 2,
        out_specs=[VMEM] * parts,
        out_shape=[jax.ShapeDtypeStruct(shape, BF16)] * parts,
        compiler_params=params(12),
        name="split_sum",
    )(kept, recv)


def owned_kernel(*refs):
    parts, (mine, fix, squares) = refs[:8], refs[8:]
    inside = lax.broadcasted_iota(jnp.int32, (PAD, LANES), 0) < UNITS
    total_sq = jnp.zeros((PAD, LANES), F32)
    for half in range(2):
        t = parts[4 * half : 4 * half + 4]
        lanes = slice(half * LANES, half * LANES + LANES)
        for m in range(3):
            for c in range(N_C):
                v = t[0][0, m, c].astype(F32) + t[1][0, m, c].astype(F32)
                v = v + (t[2][0, m, c].astype(F32) + t[3][0, m, c].astype(F32))
                total_sq += jnp.where(inside, v * v, 0.0)
                if c == 0:
                    mine[m, :, lanes] = v
                else:
                    fix[m, :, lanes] = v.astype(BF16)
    row = jnp.sum(total_sq, axis=0, keepdims=True)
    squares[...] = jnp.broadcast_to(row, squares.shape)


def owned_sum(by_x, by_z, peers):
    return pl.pallas_call(
        owned_kernel,
        in_specs=[VMEM] * 8,
        out_specs=[VMEM] * 3,
        out_shape=[
            jax.ShapeDtypeStruct((3, PAD, 2 * LANES), F32),
            jax.ShapeDtypeStruct((3, PAD, 2 * LANES), BF16),
            jax.ShapeDtypeStruct((peers, LANES), F32),
        ],
        compiler_params=params(12),
        name="owned_sum",
    )(*by_x, *by_z)


def update_kernel(
    limit_sq, window, place, squares, mine, recv, first, second, b_hbm, new_first, new_second, out, b, way, sem
):
    pieces = sem.shape[1]
    wide = b.shape[1] // pieces
    jobs = [(j, m) for j in range(pieces) for m in range(3)]

    def copy(job):
        j, m = job
        at = pl.ds(j * wide, wide)
        return pltpu.make_async_copy(b_hbm.at[m, at], b.at[m, at], sem.at[m, j])

    for job in jobs[:window]:
        copy(job).start()

    total = jnp.sum(squares[...])
    clip_limit = jnp.sqrt(jnp.full((1, 1), limit_sq, F32))
    factor = jnp.minimum(1.0, clip_limit / jnp.sqrt(jnp.full((1, 1), total, F32)))
    low = place[8] == 0
    for m in range(3):
        here = mine[m]
        there = recv[m].astype(F32)
        lower = jnp.where(low, here, there)
        upper = jnp.where(low, there, here)
        clipped = jnp.concatenate([lower, upper], axis=1)[:UNITS] * factor
        one = 0.9 * first[m] + 0.1 * clipped
        two = 0.95 * second[m] + 0.05 * clipped * clipped
        new_first[m] = one
        new_second[m] = two
        turn = one / (1.0 - 0.9**STEP) / (jnp.sqrt(two / (1.0 - 0.95**STEP)) + 1e-08)
        rows = way.shape[1] - UNITS
        padded = jnp.concatenate([turn, jnp.zeros((rows, turn.shape[1]), F32)], axis=0)
        way[m] = padded.astype(BF16)

    for i, (j, m) in enumerate(jobs):
        copy((j, m)).wait()
        if i + window < len(jobs):
            copy(jobs[i + window]).start()
        full = lax.dot_general(
            way[m], b[m, j * wide : (j + 1) * wide], (((1,), (1,)), ((), ())), preferred_element_type=F32
        ).astype(BF16)
        for n in range(wide // LANES):
            out[j * (wide // LANES) + n, m] = full[:, n * LANES : (n + 1) * LANES]


def update(limit_sq, place, squares, mine, recv, first, second, bases):
    _, width, rank = bases.shape
    moment = jax.ShapeDtypeStruct((3, UNITS, rank), F32)
    return pl.pallas_call(
        functools.partial(update_kernel, limit_sq, 8),
        in_specs=[SMEM] + [VMEM] * 5 + [ANY],
        out_specs=[VMEM] * 3,
        out_shape=[
            moment,
            moment,
            jax.ShapeDtypeStruct((width // LANES, 3, PAD, LANES), BF16),
        ],
        scratch_shapes=[
            pltpu.VMEM((3, width, rank), BF16),
            pltpu.VMEM((3, PAD, rank), BF16),
            pltpu.SemaphoreType.DMA((3, 8)),
        ],
        compiler_params=params(48),
        name="update",
    )(place, squares, mine, recv, first, second, bases)


def layout_kernel(pieces, gate, up, down, rows):
    units = N_DP * UNITS
    for m, out in enumerate((gate, up, down)):
        for k in range(N_DP):
            rows[m, k * UNITS : k * UNITS + PAD, :] = pieces[k, m].astype(F32)
        out[...] = rows[m, :units, :].astype(BF16)


def layout(pieces):
    units = N_DP * UNITS
    return pl.pallas_call(
        layout_kernel,
        in_specs=[VMEM],
        out_specs=[VMEM] * 3,
        out_shape=[jax.ShapeDtypeStruct((units, LANES), BF16)] * 3,
        scratch_shapes=[pltpu.VMEM((3, units + 8, LANES), F32)],
        compiler_params=params(24),
        name="layout",
    )(pieces)


def body(activations, gate_up_grads, hidden_act, down_out_grad, bases, first_moment, second_moment):
    devices = lax.axis_size("dp") * lax.axis_size("tensor")
    total_units = hidden_act.shape[1] * lax.axis_size("tensor")
    me = lax.axis_index("dp")
    place = lax.dynamic_index_in_dim(jnp.asarray(PLACES), me, keepdims=False)

    gate_up = jnp.swapaxes(gate_up_grads, 1, 2)
    hidden = hidden_act.T[None]
    gate_up_there = lax.ppermute(gate_up, "dp", CORE_PAIRS)
    hidden_there = lax.ppermute(hidden, "dp", CORE_PAIRS)
    kept, sent = project(place, activations, down_out_grad, bases)
    theirs = lax.ppermute(sent, "dp", CORE_PAIRS)
    xa, xb, za, zb = collect(place, gate_up, hidden, gate_up_there, hidden_there, kept, theirs)

    xr = lax.ppermute(xb, "dp", along_x(0))
    zr = lax.ppermute(zb, "dp", along_z(0))
    xa, xb = split_sum(xa, xr, 2)
    za, zb = split_sum(za, zr, 2)
    xr = lax.ppermute(xb, "dp", along_x(1))
    zr = lax.ppermute(zb, "dp", along_z(1))
    by_x = split_sum(xa[0], xr[0], 4)
    by_z = split_sum(za[0], zr[0], 4)
    by_x = [by_x[0]] + [lax.ppermute(by_x[r], "dp", direct_z(r)) for r in (1, 2, 3)]
    by_z = [by_z[0]] + [lax.ppermute(by_z[r], "dp", direct_x(r)) for r in (1, 2, 3)]
    mine, fix, squares = owned_sum(by_x, by_z, devices)
    fix = lax.ppermute(fix, "dp", CORE_PAIRS)
    squares = lax.all_to_all(squares, ("dp", "tensor"), 0, 0, tiled=True)

    limit_sq = float(3 * bases.shape[2] * total_units)
    new_first, new_second, pieces = update(
        limit_sq, place, squares, mine, fix, first_moment[:, 0], second_moment[:, 0], bases
    )
    pieces = lax.all_to_all(pieces, "dp", 0, 0, tiled=True)
    gate_update, up_update, down_update = layout(pieces)
    return (gate_update.T, up_update.T, down_update, new_first[:, None], new_second[:, None])


def solution(mesh):
    placed = (
        P("dp", None),
        P(None, "dp", "tensor"),
        P("dp", "tensor"),
        P("dp", None),
        P(),
        P(None, "tensor", "dp", None),
        P(None, "tensor", "dp", None),
    )
    return jax.shard_map(
        body,
        mesh=mesh,
        in_specs=placed,
        out_specs=(
            P("dp", "tensor"),
            P("dp", "tensor"),
            P("tensor", "dp"),
            P(None, "tensor", "dp", None),
            P(None, "tensor", "dp", None),
        ),
        check_vma=False,
    )
```

```python
import functools

import jax
import jax.numpy as jnp
from jax import lax
from jax.experimental import pallas as pl
from jax.experimental.pallas import tpu as pltpu
from jax.sharding import PartitionSpec as P

STEP = 10
N_Z, N_X, N_C = 4, 4, 2
N_DP = N_Z * N_X * N_C
UNITS = 86
PAD = 88
LANES = 128
BF16 = jnp.bfloat16
F32 = jnp.float32
MB = 1 << 20


def dp_index(z, x, c):
    return ((z % N_Z) * N_X + (x % N_X)) * N_C + c % N_C


def every_chip():
    return [(z, x, c) for z in range(N_Z) for x in range(N_X) for c in range(N_C)]


CORE_PAIRS = [(dp_index(z, x, c), dp_index(z, x, c + 1)) for z, x, c in every_chip()]


FLIPS = ((1, 3), (3, 1))
FLIP_ORDER = tuple((0, b, a, a ^ b) for a, b in FLIPS)


def along_x(turn):
    return [(dp_index(z, x, c), dp_index(z, x ^ FLIPS[c][turn], c)) for z, x, c in every_chip()]


def along_z(turn):
    return [(dp_index(z, x, c), dp_index(z ^ FLIPS[c][turn], x, c)) for z, x, c in every_chip()]


def direct_x(r):
    return [(dp_index(z, x, c), dp_index(z, x ^ FLIP_ORDER[c][r], c)) for z, x, c in every_chip()]


def direct_z(r):
    return [(dp_index(z, x, c), dp_index(z ^ FLIP_ORDER[c][r], x, c)) for z, x, c in every_chip()]


def my_place():
    me = lax.axis_index("dp")
    z = lax.shift_right_logical(me, 3)
    x = lax.bitwise_and(lax.shift_right_logical(me, 1), 3)
    return z, x, lax.bitwise_and(me, 1)


def my_core():
    return my_place()[2]


def turned(offset):
    return jnp.where(my_core() == 0, lax.bitwise_and(4 - offset, 3), offset)


def flip_order(r):
    return turned(lax.bitwise_xor(r, lax.shift_right_logical(r, 1)))


def rank_of(offset):
    at = turned(offset)
    return lax.bitwise_xor(at, lax.shift_right_logical(at, 1))


VMEM = pl.BlockSpec(memory_space=pltpu.VMEM)
ANY = pl.BlockSpec(memory_space=pl.ANY)


def params(mib, **more):
    return pltpu.CompilerParams(vmem_limit_bytes=mib * MB, **more)


def project_kernel(first, steps, window, x_hbm, b_hbm, kept, sent, x, b, acc, sem_a, sem_b):
    count = acc.shape[0]
    wide = x.shape[1] // steps
    half = kept.shape[2]

    def copies(k):
        at = pl.ds(k * wide, wide)
        yield pltpu.make_async_copy(x_hbm.at[:, at], x.at[:, at], sem_a.at[k])
        for m in range(count):
            yield pltpu.make_async_copy(b_hbm.at[first + m, at], b.at[m, at], sem_b.at[m, k])

    for k in range(window):
        for copy in copies(k):
            copy.start()
    for k in range(steps):
        for copy in copies(k):
            copy.wait()
        if k + window < steps:
            for copy in copies(k + window):
                copy.start()
        at = slice(k * wide, (k + 1) * wide)
        for m in range(count):
            part = jnp.dot(x[:, at], b[m, at], preferred_element_type=F32)
            if k == 0:
                acc[m] = part
            elif k < steps - 1:
                acc[m] += part
            else:
                full = (acc[m] + part).astype(BF16)
                low, high = full[:, :half], full[:, half:]
                lower = my_core() == 0
                kept[m] = jnp.where(lower, low, high)
                sent[m] = jnp.where(lower, high, low)


def project(x, bases, first, count):
    tokens, width = x.shape
    rank = bases.shape[2]
    steps = 8
    out = jax.ShapeDtypeStruct((count, tokens, rank // 2), BF16)
    return pl.pallas_call(
        functools.partial(project_kernel, first, steps, 4),
        in_specs=[ANY, ANY],
        out_specs=[VMEM] * 2,
        out_shape=[out, out],
        scratch_shapes=[
            pltpu.VMEM((tokens, width), BF16),
            pltpu.VMEM((count, width, rank), BF16),
            pltpu.VMEM((count, tokens, rank), F32),
            pltpu.SemaphoreType.DMA((steps,)),
            pltpu.SemaphoreType.DMA((count, steps)),
        ],
        compiler_params=params(58),
        cost_estimate=pl.CostEstimate(
            flops=2 * count * tokens * rank * width,
            bytes_accessed=2 * (tokens * width + count * width * rank),
            transcendentals=0,
        ),
        name="project",
    )(x, bases)


PIECES_TWO = ((("x", 0), ("x", 1)), (("x", 2), ("z", 2)))
PIECES_ONE = ((("z", 0), ("z", 1)),)


def collect_kernel(pieces, g, h, mine, theirs, *refs):
    *outs, terms, cut_x, cut_z = refs
    step = pl.program_id(0)
    _, x0, c0 = my_place()
    block = g.shape[1]

    @pl.when(step == 0)
    def _():
        terms[...] = jnp.zeros(terms.shape, F32)

    z_pieces = cut_z.shape[1]
    for m, halves in enumerate(pieces):
        terms[m, :block] = jnp.dot(g[m], mine[m], preferred_element_type=F32) + jnp.dot(
            h[m], theirs[m], preferred_element_type=F32
        )
        for x in range(N_X):
            at = rank_of(lax.bitwise_xor(x0, x))
            for c in range(N_C):
                own = lax.bitwise_xor(c0, c)
                d = (x * N_C + c) * UNITS
                both = terms[m, d : d + PAD].astype(BF16)
                for half, (flow, piece) in enumerate(halves):
                    part = both[:, half * LANES : (half + 1) * LANES]
                    if flow == "x":
                        cut_x[at, piece, own] = part
                    else:
                        cut_z[at, piece % z_pieces, own] = part
    if len(outs) == 4:
        outs[0][:, 0] = cut_x[:2]
        outs[1][:, 0] = cut_x[2:]
    za, zb = outs[-2:]

    @pl.when(step < 2)
    def _():
        za[0] = cut_z[...]

    @pl.when(step >= 2)
    def _():
        zb[0] = cut_z[...]


def collect(pieces, g, h, mine, theirs):
    count, units, tokens = g.shape
    half = mine.shape[2]
    block = units // N_Z
    array = lambda count: jax.ShapeDtypeStruct((2, 4, count, N_C, PAD, LANES), BF16)
    z_of = lambda i: lax.bitwise_xor(my_place()[0], flip_order(i))
    by_z = pl.BlockSpec((count, block, tokens), lambda i: (0, z_of(i), 0))
    whole = pl.BlockSpec((count, tokens, half), lambda i: (0, 0, 0))
    x_spec = pl.BlockSpec((2, 1, 3, N_C, PAD, LANES), lambda i: (0, i, 0, 0, 0, 0))
    z_pieces = sum(flow == "z" for halves in pieces for flow, _ in halves)
    both = len(pieces) > 1
    z_shape = (1, 4, z_pieces, N_C, PAD, LANES)
    z_specs = [
        pl.BlockSpec(z_shape, lambda i: (jnp.minimum(i, 1), 0, 0, 0, 0, 0)),
        pl.BlockSpec(z_shape, lambda i: (jnp.maximum(i - 2, 0), 0, 0, 0, 0, 0)),
    ]
    out_specs = [x_spec, x_spec, *z_specs] if both else z_specs
    out_shape = [array(3)] * 2 * both + [array(z_pieces)] * 2
    return pl.pallas_call(
        functools.partial(collect_kernel, pieces),
        grid=(N_Z,),
        in_specs=[by_z, by_z, whole, whole],
        out_specs=out_specs,
        scratch_shapes=[
            pltpu.VMEM((count, block + 8, half), F32),
            pltpu.VMEM((4, 3, N_C, PAD, LANES), BF16),
            pltpu.VMEM((4, z_pieces, N_C, PAD, LANES), BF16),
        ],
        out_shape=out_shape,
        compiler_params=params(24),
        cost_estimate=pl.CostEstimate(
            flops=2 * count * 2 * tokens * units * half,
            bytes_accessed=2 * count * units * (2 * tokens + half),
            transcendentals=0,
        ),
        name="collect",
    )(g, h, mine, theirs)


def split_kernel(count, *refs):
    outs = refs[2 * count :]
    n = refs[0].shape[0] // len(outs)
    for i, out in enumerate(outs):
        at = slice(i * n, (i + 1) * n)
        piece = 0
        for kept, recv in zip(refs[:count], refs[count : 2 * count]):
            more = kept.shape[-4]
            total = (kept[at].astype(F32) + recv[at].astype(F32)).astype(BF16)
            if count == 1:
                out[...] = total
            else:
                out[:, :, piece : piece + more] = total
            piece += more


def split_sum(kept, recv, parts):
    first = kept[0].shape
    pieces = sum(t.shape[-4] for t in kept)
    shape = (first[0] // parts, *first[1:-4], pieces, *first[-3:])
    return pl.pallas_call(
        functools.partial(split_kernel, len(kept)),
        in_specs=[VMEM] * 2 * len(kept),
        out_specs=[VMEM] * parts,
        out_shape=[jax.ShapeDtypeStruct(shape, BF16)] * parts,
        compiler_params=params(12),
        name="split_sum",
    )(*kept, *recv)


def owned_kernel(*refs):
    parts, (mine, fix, squares) = refs[:8], refs[8:]
    inside = lax.broadcasted_iota(jnp.int32, (PAD, LANES), 0) < UNITS
    total_sq = jnp.zeros((PAD, LANES), F32)
    for m, halves in enumerate(PIECES_TWO + PIECES_ONE):
        for half, (flow, piece) in enumerate(halves):
            t = parts[:4] if flow == "x" else parts[4:]
            lanes = slice(half * LANES, half * LANES + LANES)
            for c in range(N_C):
                v = t[0][0, piece, c].astype(F32) + t[1][0, piece, c].astype(F32)
                v = v + (t[2][0, piece, c].astype(F32) + t[3][0, piece, c].astype(F32))
                total_sq += jnp.where(inside, v * v, 0.0)
                if c == 0:
                    mine[m, :, lanes] = v
                else:
                    fix[m, :, lanes] = v.astype(BF16)
    row = jnp.sum(total_sq, axis=0, keepdims=True)
    squares[...] = jnp.broadcast_to(row, squares.shape)


def owned_sum(by_x, by_z, peers):
    return pl.pallas_call(
        owned_kernel,
        in_specs=[VMEM] * 8,
        out_specs=[VMEM] * 3,
        out_shape=[
            jax.ShapeDtypeStruct((3, PAD, 2 * LANES), F32),
            jax.ShapeDtypeStruct((3, PAD, 2 * LANES), BF16),
            jax.ShapeDtypeStruct((peers, LANES), F32),
        ],
        compiler_params=params(12),
        name="owned_sum",
    )(*by_x, *by_z)


def update_kernel(limit_sq, squares, mine, recv, first, second, b, new_first, new_second, out, way):
    @pl.when(pl.program_id(0) == 0)
    def _():
        total = jnp.sum(squares[...])
        clip_limit = jnp.sqrt(jnp.full((1, 1), limit_sq, F32))
        factor = jnp.minimum(1.0, clip_limit / jnp.sqrt(jnp.full((1, 1), total, F32)))
        low = my_core() == 0
        for m in range(3):
            near = mine[m]
            far = recv[m].astype(F32)
            lower = jnp.where(low, near, far)
            upper = jnp.where(low, far, near)
            clipped = jnp.concatenate([lower, upper], axis=1)[:UNITS] * factor
            one = 0.9 * first[m] + 0.1 * clipped
            two = 0.95 * second[m] + 0.05 * clipped * clipped
            new_first[m] = one
            new_second[m] = two
            turn = one / (1.0 - 0.9**STEP) / (jnp.sqrt(two / (1.0 - 0.95**STEP)) + 1e-08)
            padded = jnp.concatenate([turn, jnp.zeros((PAD - UNITS, turn.shape[1]), F32)], axis=0)
            way[m] = padded.astype(BF16)

    for m in range(3):
        full = lax.dot_general(
            way[m], b[m], (((1,), (1,)), ((), ())), preferred_element_type=F32
        ).astype(BF16)
        for n in range(out.shape[0]):
            out[n, m] = full[:, n * LANES : (n + 1) * LANES]


def update(limit_sq, squares, mine, recv, first, second, bases):
    _, width, rank = bases.shape
    steps = 4
    moment = jax.ShapeDtypeStruct((3, UNITS, rank), F32)
    whole = lambda array: pl.BlockSpec(array.shape, lambda i: (0,) * array.ndim)
    inputs = (squares, mine, recv, first, second)
    owners = width // LANES
    return pl.pallas_call(
        functools.partial(update_kernel, limit_sq),
        grid=(steps,),
        in_specs=[whole(t) for t in inputs]
        + [pl.BlockSpec((3, width // steps, rank), lambda i: (0, i, 0))],
        out_specs=[
            whole(moment),
            whole(moment),
            pl.BlockSpec((owners // steps, 3, PAD, LANES), lambda i: (i, 0, 0, 0)),
        ],
        out_shape=[moment, moment, jax.ShapeDtypeStruct((owners, 3, PAD, LANES), BF16)],
        scratch_shapes=[pltpu.VMEM((3, PAD, rank), BF16)],
        compiler_params=params(52),
        name="update",
    )(*inputs, bases)


def layout_kernel(pieces, gate, up, down, rows):
    units = N_DP * UNITS
    for m, out in enumerate((gate, up, down)):
        for k in range(N_DP):
            rows[m, k * UNITS : k * UNITS + PAD, :] = pieces[k, m].astype(F32)
        out[...] = rows[m, :units, :].astype(BF16)


def layout(pieces):
    units = N_DP * UNITS
    return pl.pallas_call(
        layout_kernel,
        in_specs=[VMEM],
        out_specs=[VMEM] * 3,
        out_shape=[jax.ShapeDtypeStruct((units, LANES), BF16)] * 3,
        scratch_shapes=[pltpu.VMEM((3, units + 8, LANES), F32)],
        compiler_params=params(24),
        name="layout",
    )(pieces)


def body(activations, gate_up_grads, hidden_act, down_out_grad, bases, first_moment, second_moment):
    devices = lax.axis_size("dp") * lax.axis_size("tensor")
    total_units = hidden_act.shape[1] * lax.axis_size("tensor")
    gate_up = jnp.swapaxes(gate_up_grads, 1, 2)
    hidden = hidden_act.T[None]
    gate_up_there = lax.ppermute(gate_up, "dp", CORE_PAIRS)
    hidden_there = lax.ppermute(hidden, "dp", CORE_PAIRS)
    kept_two, sent_two = project(activations, bases, 0, 2)
    theirs_two = lax.ppermute(sent_two, "dp", CORE_PAIRS)
    kept_one, sent_one = project(down_out_grad, bases, 2, 1)
    theirs_one = lax.ppermute(sent_one, "dp", CORE_PAIRS)
    xa, xb, za_one, zb_one = collect(PIECES_TWO, gate_up, gate_up_there, kept_two, theirs_two)
    xr = lax.ppermute(xb, "dp", along_x(0))
    zr_one = lax.ppermute(zb_one, "dp", along_z(0))
    za_two, zb_two = collect(PIECES_ONE, hidden, hidden_there, kept_one, theirs_one)
    zr_two = lax.ppermute(zb_two, "dp", along_z(0))

    xa, xb = split_sum([xa], [xr], 2)
    za_one, za_two, xb = lax.optimization_barrier((za_one, za_two, xb))
    xr = lax.ppermute(xb, "dp", along_x(1))
    za, zb = split_sum([za_two, za_one], [zr_two, zr_one], 2)
    zr = lax.ppermute(zb, "dp", along_z(1))
    by_x = split_sum([xa[0]], [xr[0]], 4)
    za, *by_x = lax.optimization_barrier((za, *by_x))
    by_z = split_sum([za[0]], [zr[0]], 4)
    by_x = [by_x[0]] + [lax.ppermute(by_x[r], "dp", direct_z(r)) for r in (1, 2, 3)]
    by_z = [by_z[0]] + [lax.ppermute(by_z[r], "dp", direct_x(r)) for r in (1, 2, 3)]
    mine, fix, squares = owned_sum(by_x, by_z, devices)
    fix = lax.ppermute(fix, "dp", CORE_PAIRS)
    squares = lax.all_to_all(squares, ("dp", "tensor"), 0, 0, tiled=True)

    limit_sq = float(3 * bases.shape[2] * total_units)
    new_first, new_second, pieces = update(
        limit_sq, squares, mine, fix, first_moment[:, 0], second_moment[:, 0], bases
    )
    pieces = lax.all_to_all(pieces, "dp", 0, 0, tiled=True)
    gate_update, up_update, down_update = layout(pieces)
    return (gate_update.T, up_update.T, down_update, new_first[:, None], new_second[:, None])


def solution(mesh):
    placed = (
        P("dp", None),
        P(None, "dp", "tensor"),
        P("dp", "tensor"),
        P("dp", None),
        P(),
        P(None, "tensor", "dp", None),
        P(None, "tensor", "dp", None),
    )
    return jax.shard_map(
        body,
        mesh=mesh,
        in_specs=placed,
        out_specs=(
            P("dp", "tensor"),
            P("dp", "tensor"),
            P("tensor", "dp"),
            P(None, "tensor", "dp", None),
            P(None, "tensor", "dp", None),
        ),
        check_vma=False,
    )
```

```python
import functools

import jax
import jax.numpy as jnp
from jax import lax
from jax.experimental import pallas as pl
from jax.experimental.pallas import tpu as pltpu
from jax.sharding import PartitionSpec as P

STEP = 10
N_Z, N_X, N_C = 4, 4, 2
N_DP = N_Z * N_X * N_C
UNITS = 86
PAD = 88
LANES = 128
BF16 = jnp.bfloat16
F32 = jnp.float32
MB = 1 << 20


def dp_index(z, x, c):
    return ((z % N_Z) * N_X + (x % N_X)) * N_C + c % N_C


def every_chip():
    return [(z, x, c) for z in range(N_Z) for x in range(N_X) for c in range(N_C)]


CORE_PAIRS = [(dp_index(z, x, c), dp_index(z, x, c + 1)) for z, x, c in every_chip()]


FLIPS = ((1, 3), (3, 1))
FLIP_ORDER = tuple((0, b, a, a ^ b) for a, b in FLIPS)


def along_x(turn):
    return [(dp_index(z, x, c), dp_index(z, x ^ FLIPS[c][turn], c)) for z, x, c in every_chip()]


def along_z(turn):
    return [(dp_index(z, x, c), dp_index(z ^ FLIPS[c][turn], x, c)) for z, x, c in every_chip()]


def direct_x(r):
    return [(dp_index(z, x, c), dp_index(z, x ^ FLIP_ORDER[c][r], c)) for z, x, c in every_chip()]


def direct_z(r):
    return [(dp_index(z, x, c), dp_index(z ^ FLIP_ORDER[c][r], x, c)) for z, x, c in every_chip()]


def my_place():
    me = lax.axis_index("dp")
    z = lax.shift_right_logical(me, 3)
    x = lax.bitwise_and(lax.shift_right_logical(me, 1), 3)
    return z, x, lax.bitwise_and(me, 1)


def my_core():
    return my_place()[2]


def turned(offset):
    return jnp.where(my_core() == 0, lax.bitwise_and(4 - offset, 3), offset)


def flip_order(r):
    return turned(lax.bitwise_xor(r, lax.shift_right_logical(r, 1)))


def rank_of(offset):
    at = turned(offset)
    return lax.bitwise_xor(at, lax.shift_right_logical(at, 1))


VMEM = pl.BlockSpec(memory_space=pltpu.VMEM)
ANY = pl.BlockSpec(memory_space=pl.ANY)


def params(mib, **more):
    return pltpu.CompilerParams(vmem_limit_bytes=mib * MB, **more)


def project_kernel(first, steps, window, x_hbm, b_hbm, kept, sent, x, b, acc, sem_a, sem_b):
    count = acc.shape[0]
    wide = x.shape[1] // steps
    half = kept.shape[2]

    def copies(k):
        at = pl.ds(k * wide, wide)
        yield pltpu.make_async_copy(x_hbm.at[:, at], x.at[:, at], sem_a.at[k])
        for m in range(count):
            yield pltpu.make_async_copy(b_hbm.at[first + m, at], b.at[m, at], sem_b.at[m, k])

    for k in range(window):
        for copy in copies(k):
            copy.start()
    for k in range(steps):
        for copy in copies(k):
            copy.wait()
        if k + window < steps:
            for copy in copies(k + window):
                copy.start()
        at = slice(k * wide, (k + 1) * wide)
        for m in range(count):
            part = jnp.dot(x[:, at], b[m, at], preferred_element_type=F32)
            if k == 0:
                acc[m] = part
            elif k < steps - 1:
                acc[m] += part
            else:
                full = (acc[m] + part).astype(BF16)
                low, high = full[:, :half], full[:, half:]
                lower = my_core() == 0
                kept[m] = jnp.where(lower, low, high)
                sent[m] = jnp.where(lower, high, low)


def project(x, bases, first, count):
    tokens, width = x.shape
    rank = bases.shape[2]
    steps = 8
    out = jax.ShapeDtypeStruct((count, tokens, rank // 2), BF16)
    return pl.pallas_call(
        functools.partial(project_kernel, first, steps, 8),
        in_specs=[ANY, ANY],
        out_specs=[VMEM] * 2,
        out_shape=[out, out],
        scratch_shapes=[
            pltpu.VMEM((tokens, width), BF16),
            pltpu.VMEM((count, width, rank), BF16),
            pltpu.VMEM((count, tokens, rank), F32),
            pltpu.SemaphoreType.DMA((steps,)),
            pltpu.SemaphoreType.DMA((count, steps)),
        ],
        compiler_params=params(58),
        cost_estimate=pl.CostEstimate(
            flops=2 * count * tokens * rank * width,
            bytes_accessed=2 * (tokens * width + count * width * rank),
            transcendentals=0,
        ),
        name="project",
    )(x, bases)


def collect_kernel(x_first, g, h, mine, theirs, stay, go, terms, cut):
    step = pl.program_id(0)
    _, x0, c0 = my_place()
    block = g.shape[1]

    @pl.when(step == 0)
    def _():
        terms[...] = jnp.zeros(terms.shape, F32)

    for m in range(g.shape[0]):
        terms[m, :block] = jnp.dot(g[m], mine[m], preferred_element_type=F32) + jnp.dot(
            h[m], theirs[m], preferred_element_type=F32
        )
        for x in range(N_X):
            at = rank_of(lax.bitwise_xor(x0, x))
            for c in range(N_C):
                own = lax.bitwise_xor(c0, c)
                d = (x * N_C + c) * UNITS
                both = terms[m, d : d + PAD].astype(BF16)
                cut[at, 2 * m, own] = both[:, :LANES]
                cut[at, 2 * m + 1, own] = both[:, LANES:]
    if x_first:
        stay[:, 0] = cut[:2]
        go[:, 0] = cut[2:]
        return

    @pl.when(step < 2)
    def _():
        stay[0] = cut[...]

    @pl.when(step >= 2)
    def _():
        go[0] = cut[...]


def collect(x_first, g, h, mine, theirs):
    count, units, tokens = g.shape
    half = mine.shape[2]
    block = units // N_Z
    pieces = 2 * count
    array = jax.ShapeDtypeStruct((2, 4, pieces, N_C, PAD, LANES), BF16)
    z_of = lambda i: lax.bitwise_xor(my_place()[0], flip_order(i))
    by_z = pl.BlockSpec((count, block, tokens), lambda i: (0, z_of(i), 0))
    whole = pl.BlockSpec((count, tokens, half), lambda i: (0, 0, 0))
    if x_first:
        out_specs = [pl.BlockSpec((2, 1, pieces, N_C, PAD, LANES), lambda i: (0, i, 0, 0, 0, 0))] * 2
    else:
        shape = (1, 4, pieces, N_C, PAD, LANES)
        out_specs = [
            pl.BlockSpec(shape, lambda i: (jnp.minimum(i, 1), 0, 0, 0, 0, 0)),
            pl.BlockSpec(shape, lambda i: (jnp.maximum(i - 2, 0), 0, 0, 0, 0, 0)),
        ]
    return pl.pallas_call(
        functools.partial(collect_kernel, x_first),
        grid=(N_Z,),
        in_specs=[by_z, by_z, whole, whole],
        out_specs=out_specs,
        scratch_shapes=[
            pltpu.VMEM((count, block + 8, half), F32),
            pltpu.VMEM((4, pieces, N_C, PAD, LANES), BF16),
        ],
        out_shape=[array] * 2,
        compiler_params=params(24),
        cost_estimate=pl.CostEstimate(
            flops=2 * count * 2 * tokens * units * half,
            bytes_accessed=2 * count * units * (2 * tokens + half),
            transcendentals=0,
        ),
        name="collect",
    )(g, h, mine, theirs)


def split_kernel(kept, recv, *outs):
    n = kept.shape[0] // len(outs)
    for i, out in enumerate(outs):
        at = slice(i * n, (i + 1) * n)
        out[...] = (kept[at].astype(F32) + recv[at].astype(F32)).astype(BF16)


def split_sum(kept, recv, parts):
    shape = (kept.shape[0] // parts, *kept.shape[1:])
    return pl.pallas_call(
        split_kernel,
        in_specs=[VMEM] * 2,
        out_specs=[VMEM] * parts,
        out_shape=[jax.ShapeDtypeStruct(shape, BF16)] * parts,
        compiler_params=params(12),
        name="split_sum",
    )(kept, recv)


def owned_kernel(*refs):
    parts, (mine, fix, squares) = refs[:8], refs[8:]
    inside = lax.broadcasted_iota(jnp.int32, (PAD, LANES), 0) < UNITS
    total_sq = jnp.zeros((PAD, LANES), F32)
    for m in range(3):
        for half in range(2):
            t, piece = (parts[:4], 2 * m + half) if m < 2 else (parts[4:], half)
            lanes = slice(half * LANES, half * LANES + LANES)
            for c in range(N_C):
                v = t[0][0, piece, c].astype(F32) + t[1][0, piece, c].astype(F32)
                v = v + (t[2][0, piece, c].astype(F32) + t[3][0, piece, c].astype(F32))
                total_sq += jnp.where(inside, v * v, 0.0)
                if c == 0:
                    mine[m, :, lanes] = v
                else:
                    fix[m, :, lanes] = v.astype(BF16)
    row = jnp.sum(total_sq, axis=0, keepdims=True)
    squares[...] = jnp.broadcast_to(row, squares.shape)


def owned_sum(by_x, by_z, peers):
    return pl.pallas_call(
        owned_kernel,
        in_specs=[VMEM] * 8,
        out_specs=[VMEM] * 3,
        out_shape=[
            jax.ShapeDtypeStruct((3, PAD, 2 * LANES), F32),
            jax.ShapeDtypeStruct((3, PAD, 2 * LANES), BF16),
            jax.ShapeDtypeStruct((peers, LANES), F32),
        ],
        compiler_params=params(12),
        name="owned_sum",
    )(*by_x, *by_z)


def update_kernel(
    limit_sq, squares, mine, recv, first, second, b_hbm, new_first, new_second, out, way, b, sem
):
    step = pl.program_id(0)
    wide = b.shape[2]

    def copy(j):
        return pltpu.make_async_copy(b_hbm.at[:, pl.ds(j * wide, wide)], b.at[j], sem.at[j])

    @pl.when(step == 0)
    def _():
        for j in range(b.shape[0]):
            copy(j).start()
        total = jnp.sum(squares[...])
        clip_limit = jnp.sqrt(jnp.full((1, 1), limit_sq, F32))
        factor = jnp.minimum(1.0, clip_limit / jnp.sqrt(jnp.full((1, 1), total, F32)))
        low = my_core() == 0
        for m in range(3):
            near = mine[m]
            far = recv[m].astype(F32)
            lower = jnp.where(low, near, far)
            upper = jnp.where(low, far, near)
            clipped = jnp.concatenate([lower, upper], axis=1)[:UNITS] * factor
            one = 0.9 * first[m] + 0.1 * clipped
            two = 0.95 * second[m] + 0.05 * clipped * clipped
            new_first[m] = one
            new_second[m] = two
            turn = one / (1.0 - 0.9**STEP) / (jnp.sqrt(two / (1.0 - 0.95**STEP)) + 1e-08)
            padded = jnp.concatenate([turn, jnp.zeros((PAD - UNITS, turn.shape[1]), F32)], axis=0)
            way[m] = padded.astype(BF16)

    copy(step).wait()
    for m in range(3):
        full = lax.dot_general(
            way[m], b[step, m], (((1,), (1,)), ((), ())), preferred_element_type=F32
        ).astype(BF16)
        for n in range(out.shape[0]):
            out[n, m] = full[:, n * LANES : (n + 1) * LANES]


def update(limit_sq, squares, mine, recv, first, second, bases):
    _, width, rank = bases.shape
    steps = 4
    moment = jax.ShapeDtypeStruct((3, UNITS, rank), F32)
    whole = lambda array: pl.BlockSpec(array.shape, lambda i: (0,) * array.ndim)
    inputs = (squares, mine, recv, first, second)
    owners = width // LANES
    return pl.pallas_call(
        functools.partial(update_kernel, limit_sq),
        grid=(steps,),
        in_specs=[whole(t) for t in inputs] + [ANY],
        out_specs=[
            whole(moment),
            whole(moment),
            pl.BlockSpec((owners // steps, 3, PAD, LANES), lambda i: (i, 0, 0, 0)),
        ],
        out_shape=[moment, moment, jax.ShapeDtypeStruct((owners, 3, PAD, LANES), BF16)],
        scratch_shapes=[
            pltpu.VMEM((3, PAD, rank), BF16),
            pltpu.VMEM((steps, 3, width // steps, rank), BF16),
            pltpu.SemaphoreType.DMA((steps,)),
        ],
        compiler_params=params(52),
        name="update",
    )(*inputs, bases)


def layout_kernel(pieces, gate, up, down, rows):
    units = N_DP * UNITS
    for m, out in enumerate((gate, up, down)):
        for k in range(N_DP):
            rows[m, k * UNITS : k * UNITS + PAD, :] = pieces[k, m].astype(F32)
        out[...] = rows[m, :units, :].astype(BF16)


def layout(pieces):
    units = N_DP * UNITS
    return pl.pallas_call(
        layout_kernel,
        in_specs=[VMEM],
        out_specs=[VMEM] * 3,
        out_shape=[jax.ShapeDtypeStruct((units, LANES), BF16)] * 3,
        scratch_shapes=[pltpu.VMEM((3, units + 8, LANES), F32)],
        compiler_params=params(24),
        name="layout",
    )(pieces)


def body(activations, gate_up_grads, hidden_act, down_out_grad, bases, first_moment, second_moment):
    devices = lax.axis_size("dp") * lax.axis_size("tensor")
    total_units = hidden_act.shape[1] * lax.axis_size("tensor")
    gate_up = jnp.swapaxes(gate_up_grads, 1, 2)
    hidden = hidden_act.T[None]
    gate_up_there = lax.ppermute(gate_up, "dp", CORE_PAIRS)
    hidden_there = lax.ppermute(hidden, "dp", CORE_PAIRS)
    kept_two, sent_two = project(activations, bases, 0, 2)
    theirs_two = lax.ppermute(sent_two, "dp", CORE_PAIRS)
    kept_one, sent_one = project(down_out_grad, bases, 2, 1)
    theirs_one = lax.ppermute(sent_one, "dp", CORE_PAIRS)
    kept_two, kept_one = lax.optimization_barrier((kept_two, kept_one))
    xa, xb = collect(True, gate_up, gate_up_there, kept_two, theirs_two)
    xr = lax.ppermute(xb, "dp", along_x(0))
    za, zb = collect(False, hidden, hidden_there, kept_one, theirs_one)
    zr = lax.ppermute(zb, "dp", along_z(0))
    za, zb = split_sum(za, zr, 2)
    xa, zb = lax.optimization_barrier((xa, zb))
    xa, xb = split_sum(xa, xr, 2)
    zr = lax.ppermute(zb, "dp", along_z(1))
    xr = lax.ppermute(xb, "dp", along_x(1))
    by_z = split_sum(za[0], zr[0], 4)
    by_x = split_sum(xa[0], xr[0], 4)
    by_z = [by_z[0]] + [lax.ppermute(by_z[r], "dp", direct_x(r)) for r in (1, 2, 3)]
    by_x = [by_x[0]] + [lax.ppermute(by_x[r], "dp", direct_z(r)) for r in (1, 2, 3)]
    mine, fix, squares = owned_sum(by_x, by_z, devices)
    fix = lax.ppermute(fix, "dp", CORE_PAIRS)
    squares = lax.all_to_all(squares, ("dp", "tensor"), 0, 0, tiled=True)

    limit_sq = float(3 * bases.shape[2] * total_units)
    new_first, new_second, pieces = update(
        limit_sq, squares, mine, fix, first_moment[:, 0], second_moment[:, 0], bases
    )
    pieces = lax.all_to_all(pieces, "dp", 0, 0, tiled=True)
    gate_update, up_update, down_update = layout(pieces)
    return (gate_update.T, up_update.T, down_update, new_first[:, None], new_second[:, None])


def solution(mesh):
    placed = (
        P("dp", None),
        P(None, "dp", "tensor"),
        P("dp", "tensor"),
        P("dp", None),
        P(),
        P(None, "tensor", "dp", None),
        P(None, "tensor", "dp", None),
    )
    return jax.shard_map(
        body,
        mesh=mesh,
        in_specs=placed,
        out_specs=(
            P("dp", "tensor"),
            P("dp", "tensor"),
            P("tensor", "dp"),
            P(None, "tensor", "dp", None),
            P(None, "tensor", "dp", None),
        ),
        check_vma=False,
    )
```

```python
import functools

import jax
import jax.numpy as jnp
from jax import lax
from jax.experimental import pallas as pl
from jax.experimental.pallas import tpu as pltpu
from jax.sharding import PartitionSpec as P

STEP = 10
N_Z, N_X, N_C = 4, 4, 2
N_DP = N_Z * N_X * N_C
UNITS = 86
PAD = 88
LANES = 128
BF16 = jnp.bfloat16
F32 = jnp.float32
MB = 1 << 20


def dp_index(z, x, c):
    return ((z % N_Z) * N_X + (x % N_X)) * N_C + c % N_C


def every_chip():
    return [(z, x, c) for z in range(N_Z) for x in range(N_X) for c in range(N_C)]


CORE_PAIRS = [(dp_index(z, x, c), dp_index(z, x, c + 1)) for z, x, c in every_chip()]


FLIPS = ((1, 3), (3, 1))
FLIP_ORDER = tuple((0, b, a, a ^ b) for a, b in FLIPS)


def along_x(turn):
    return [(dp_index(z, x, c), dp_index(z, x ^ FLIPS[c][turn], c)) for z, x, c in every_chip()]


def along_z(turn):
    return [(dp_index(z, x, c), dp_index(z ^ FLIPS[c][turn], x, c)) for z, x, c in every_chip()]


def direct_x(r):
    return [(dp_index(z, x, c), dp_index(z, x ^ FLIP_ORDER[c][r], c)) for z, x, c in every_chip()]


def direct_z(r):
    return [(dp_index(z, x, c), dp_index(z ^ FLIP_ORDER[c][r], x, c)) for z, x, c in every_chip()]


def my_place():
    me = lax.axis_index("dp")
    z = lax.shift_right_logical(me, 3)
    x = lax.bitwise_and(lax.shift_right_logical(me, 1), 3)
    return z, x, lax.bitwise_and(me, 1)


def my_core():
    return my_place()[2]


def turned(offset):
    return jnp.where(my_core() == 0, lax.bitwise_and(4 - offset, 3), offset)


def flip_order(r):
    return turned(lax.bitwise_xor(r, lax.shift_right_logical(r, 1)))


def rank_of(offset):
    at = turned(offset)
    return lax.bitwise_xor(at, lax.shift_right_logical(at, 1))


VMEM = pl.BlockSpec(memory_space=pltpu.VMEM)
ANY = pl.BlockSpec(memory_space=pl.ANY)


def params(mib, **more):
    return pltpu.CompilerParams(vmem_limit_bytes=mib * MB, **more)


def project_kernel(first, steps, window, x_hbm, b_hbm, kept, sent, x, b, acc, sem_a, sem_b):
    count = acc.shape[0]
    wide = x.shape[1] // steps
    half = kept.shape[2]

    def copies(k):
        at = pl.ds(k * wide, wide)
        yield pltpu.make_async_copy(x_hbm.at[:, at], x.at[:, at], sem_a.at[k])
        for m in range(count):
            yield pltpu.make_async_copy(b_hbm.at[first + m, at], b.at[m, at], sem_b.at[m, k])

    for k in range(window):
        for copy in copies(k):
            copy.start()
    for k in range(steps):
        for copy in copies(k):
            copy.wait()
        if k + window < steps:
            for copy in copies(k + window):
                copy.start()
        at = slice(k * wide, (k + 1) * wide)
        for m in range(count):
            part = jnp.dot(x[:, at], b[m, at], preferred_element_type=F32)
            if k == 0:
                acc[m] = part
            elif k < steps - 1:
                acc[m] += part
            else:
                full = (acc[m] + part).astype(BF16)
                low, high = full[:, :half], full[:, half:]
                lower = my_core() == 0
                kept[m] = jnp.where(lower, low, high)
                sent[m] = jnp.where(lower, high, low)


def project(x, bases, first, count, window):
    tokens, width = x.shape
    rank = bases.shape[2]
    steps = 8
    out = jax.ShapeDtypeStruct((count, tokens, rank // 2), BF16)
    return pl.pallas_call(
        functools.partial(project_kernel, first, steps, window),
        in_specs=[ANY, ANY],
        out_specs=[VMEM] * 2,
        out_shape=[out, out],
        scratch_shapes=[
            pltpu.VMEM((tokens, width), BF16),
            pltpu.VMEM((count, width, rank), BF16),
            pltpu.VMEM((count, tokens, rank), F32),
            pltpu.SemaphoreType.DMA((steps,)),
            pltpu.SemaphoreType.DMA((count, steps)),
        ],
        compiler_params=params(58),
        cost_estimate=pl.CostEstimate(
            flops=2 * count * tokens * rank * width,
            bytes_accessed=2 * (tokens * width + count * width * rank),
            transcendentals=0,
        ),
        name="project",
    )(x, bases)


def collect_kernel(x_first, g, h, mine, theirs, stay, go, terms, cut):
    step = pl.program_id(0)
    _, x0, c0 = my_place()
    block = g.shape[1]

    @pl.when(step == 0)
    def _():
        terms[...] = jnp.zeros(terms.shape, F32)

    for m in range(g.shape[0]):
        terms[m, :block] = jnp.dot(g[m], mine[m], preferred_element_type=F32) + jnp.dot(
            h[m], theirs[m], preferred_element_type=F32
        )
        for x in range(N_X):
            at = rank_of(lax.bitwise_xor(x0, x))
            for c in range(N_C):
                own = lax.bitwise_xor(c0, c)
                d = (x * N_C + c) * UNITS
                both = terms[m, d : d + PAD].astype(BF16)
                cut[at, 2 * m, own] = both[:, :LANES]
                cut[at, 2 * m + 1, own] = both[:, LANES:]
    if x_first:
        stay[:, 0] = cut[:2]
        go[:, 0] = cut[2:]
        return

    @pl.when(step < 2)
    def _():
        stay[0] = cut[...]

    @pl.when(step >= 2)
    def _():
        go[0] = cut[...]


def collect(x_first, g, h, mine, theirs):
    count, units, tokens = g.shape
    half = mine.shape[2]
    block = units // N_Z
    pieces = 2 * count
    array = jax.ShapeDtypeStruct((2, 4, pieces, N_C, PAD, LANES), BF16)
    z_of = lambda i: lax.bitwise_xor(my_place()[0], flip_order(i))
    by_z = pl.BlockSpec((count, block, tokens), lambda i: (0, z_of(i), 0))
    whole = pl.BlockSpec((count, tokens, half), lambda i: (0, 0, 0))
    if x_first:
        out_specs = [pl.BlockSpec((2, 1, pieces, N_C, PAD, LANES), lambda i: (0, i, 0, 0, 0, 0))] * 2
    else:
        shape = (1, 4, pieces, N_C, PAD, LANES)
        out_specs = [
            pl.BlockSpec(shape, lambda i: (jnp.minimum(i, 1), 0, 0, 0, 0, 0)),
            pl.BlockSpec(shape, lambda i: (jnp.maximum(i - 2, 0), 0, 0, 0, 0, 0)),
        ]
    return pl.pallas_call(
        functools.partial(collect_kernel, x_first),
        grid=(N_Z,),
        in_specs=[by_z, by_z, whole, whole],
        out_specs=out_specs,
        scratch_shapes=[
            pltpu.VMEM((count, block + 8, half), F32),
            pltpu.VMEM((4, pieces, N_C, PAD, LANES), BF16),
        ],
        out_shape=[array] * 2,
        compiler_params=params(24),
        cost_estimate=pl.CostEstimate(
            flops=2 * count * 2 * tokens * units * half,
            bytes_accessed=2 * count * units * (2 * tokens + half),
            transcendentals=0,
        ),
        name="collect",
    )(g, h, mine, theirs)


def split_kernel(kept, recv, *outs):
    n = kept.shape[0] // len(outs)
    for i, out in enumerate(outs):
        at = slice(i * n, (i + 1) * n)
        out[...] = (kept[at].astype(F32) + recv[at].astype(F32)).astype(BF16)


def split_sum(kept, recv, parts):
    shape = (kept.shape[0] // parts, *kept.shape[1:])
    return pl.pallas_call(
        split_kernel,
        in_specs=[VMEM] * 2,
        out_specs=[VMEM] * parts,
        out_shape=[jax.ShapeDtypeStruct(shape, BF16)] * parts,
        compiler_params=params(12),
        name="split_sum",
    )(kept, recv)


def owned_kernel(*refs):
    parts, (mine, fix, squares) = refs[:-3], refs[-3:]
    inside = lax.broadcasted_iota(jnp.int32, (PAD, LANES), 0) < UNITS
    total_sq = jnp.zeros((PAD, LANES), F32)
    for m in range(3):
        for half in range(2):
            t, piece = (parts[:4], 2 * m + half) if m < 2 else (parts[4:], half)
            lanes = slice(half * LANES, half * LANES + LANES)
            for c in range(N_C):
                v = sum(u[0, piece, c].astype(F32) for u in t)
                total_sq += jnp.where(inside, v * v, 0.0)
                if c == 0:
                    mine[m, :, lanes] = v
                else:
                    fix[m, :, lanes] = v.astype(BF16)
    row = jnp.sum(total_sq, axis=0, keepdims=True)
    squares[...] = jnp.broadcast_to(row, squares.shape)


def owned_sum(by_x, by_z, peers):
    return pl.pallas_call(
        owned_kernel,
        in_specs=[VMEM] * len((*by_x, *by_z)),
        out_specs=[VMEM] * 3,
        out_shape=[
            jax.ShapeDtypeStruct((3, PAD, 2 * LANES), F32),
            jax.ShapeDtypeStruct((3, PAD, 2 * LANES), BF16),
            jax.ShapeDtypeStruct((peers, LANES), F32),
        ],
        compiler_params=params(12),
        name="owned_sum",
    )(*by_x, *by_z)


def update_kernel(
    limit_sq, squares, mine, recv, first, second, b_hbm, new_first, new_second, out, way, b, sem
):
    step = pl.program_id(0)
    wide = b.shape[2]

    def copy(j):
        return pltpu.make_async_copy(b_hbm.at[:, pl.ds(j * wide, wide)], b.at[j], sem.at[j])

    @pl.when(step == 0)
    def _():
        for j in range(b.shape[0]):
            copy(j).start()
        total = jnp.sum(squares[...])
        clip_limit = jnp.sqrt(jnp.full((1, 1), limit_sq, F32))
        factor = jnp.minimum(1.0, clip_limit / jnp.sqrt(jnp.full((1, 1), total, F32)))
        low = my_core() == 0
        for m in range(3):
            near = mine[m]
            far = recv[m].astype(F32)
            lower = jnp.where(low, near, far)
            upper = jnp.where(low, far, near)
            clipped = jnp.concatenate([lower, upper], axis=1)[:UNITS] * factor
            one = 0.9 * first[m] + 0.1 * clipped
            two = 0.95 * second[m] + 0.05 * clipped * clipped
            new_first[m] = one
            new_second[m] = two
            turn = one / (1.0 - 0.9**STEP) / (jnp.sqrt(two / (1.0 - 0.95**STEP)) + 1e-08)
            padded = jnp.concatenate([turn, jnp.zeros((PAD - UNITS, turn.shape[1]), F32)], axis=0)
            way[m] = padded.astype(BF16)

    copy(step).wait()
    for m in range(3):
        full = lax.dot_general(
            way[m], b[step, m], (((1,), (1,)), ((), ())), preferred_element_type=F32
        ).astype(BF16)
        for n in range(out.shape[0]):
            out[n, m] = full[:, n * LANES : (n + 1) * LANES]


def update(limit_sq, squares, mine, recv, first, second, bases):
    _, width, rank = bases.shape
    steps = 4
    moment = jax.ShapeDtypeStruct((3, UNITS, rank), F32)
    whole = lambda array: pl.BlockSpec(array.shape, lambda i: (0,) * array.ndim)
    inputs = (squares, mine, recv, first, second)
    owners = width // LANES
    return pl.pallas_call(
        functools.partial(update_kernel, limit_sq),
        grid=(steps,),
        in_specs=[whole(t) for t in inputs] + [ANY],
        out_specs=[
            whole(moment),
            whole(moment),
            pl.BlockSpec((owners // steps, 3, PAD, LANES), lambda i: (i, 0, 0, 0)),
        ],
        out_shape=[moment, moment, jax.ShapeDtypeStruct((owners, 3, PAD, LANES), BF16)],
        scratch_shapes=[
            pltpu.VMEM((3, PAD, rank), BF16),
            pltpu.VMEM((steps, 3, width // steps, rank), BF16),
            pltpu.SemaphoreType.DMA((steps,)),
        ],
        compiler_params=params(52),
        name="update",
    )(*inputs, bases)


def layout_kernel(pieces, gate, up, down, rows, done, sem):
    units = N_DP * UNITS
    copies = []
    for m, out in enumerate((gate, up, down)):
        for k in range(N_DP):
            rows[m, k * UNITS : k * UNITS + PAD, :] = pieces[k, m].astype(F32)
        done[m] = rows[m, :units, :].astype(BF16)
        copies.append(pltpu.make_async_copy(done.at[m], out, sem.at[m]))
        copies[-1].start()
    for copy in copies:
        copy.wait()


def layout(pieces):
    units = N_DP * UNITS
    return pl.pallas_call(
        layout_kernel,
        in_specs=[VMEM],
        out_specs=[ANY] * 3,
        out_shape=[jax.ShapeDtypeStruct((units, LANES), BF16)] * 3,
        scratch_shapes=[
            pltpu.VMEM((3, units + 8, LANES), F32),
            pltpu.VMEM((3, units, LANES), BF16),
            pltpu.SemaphoreType.DMA((3,)),
        ],
        compiler_params=params(24),
        name="layout",
    )(pieces)


def body(activations, gate_up_grads, hidden_act, down_out_grad, bases, first_moment, second_moment):
    devices = lax.axis_size("dp") * lax.axis_size("tensor")
    total_units = hidden_act.shape[1] * lax.axis_size("tensor")
    gate_up = jnp.swapaxes(gate_up_grads, 1, 2)
    hidden = hidden_act.T[None]
    gate_up_there = lax.ppermute(gate_up, "dp", CORE_PAIRS)
    kept_two, sent_two = project(activations, bases, 0, 2, 4)
    theirs_two = lax.ppermute(sent_two, "dp", CORE_PAIRS)
    kept_one, sent_one = project(down_out_grad, bases, 2, 1, 8)
    theirs_one = lax.ppermute(sent_one, "dp", CORE_PAIRS)
    kept_two, kept_one, theirs_two, later = lax.optimization_barrier(
        (kept_two, kept_one, theirs_two, hidden)
    )
    hidden_there = lax.ppermute(later, "dp", CORE_PAIRS)
    xa, xb = collect(True, gate_up, gate_up_there, kept_two, theirs_two)
    xr = lax.ppermute(xb, "dp", along_x(0))
    za, zb = collect(False, hidden, hidden_there, kept_one, theirs_one)
    zr = lax.ppermute(zb, "dp", along_z(0))
    za, zb = split_sum(za, zr, 2)
    xa, zb = lax.optimization_barrier((xa, zb))
    xa, xb = split_sum(xa, xr, 2)
    zr = lax.ppermute(zb, "dp", along_z(1))
    xr = lax.ppermute(xb, "dp", along_x(1))
    za, zb = split_sum(za[0], zr[0], 2)
    zr = lax.ppermute(zb, "dp", along_x(0))
    za, zb = split_sum(za, zr, 2)
    by_x = split_sum(xa[0], xr[0], 4)
    by_z = [za, lax.ppermute(zb, "dp", along_x(1))]
    by_x = [by_x[0]] + [lax.ppermute(by_x[r], "dp", direct_z(r)) for r in (1, 2, 3)]
    mine, fix, squares = owned_sum(by_x, by_z, devices)
    fix = lax.ppermute(fix, "dp", CORE_PAIRS)
    squares = lax.all_to_all(squares, ("dp", "tensor"), 0, 0, tiled=True)

    limit_sq = float(3 * bases.shape[2] * total_units)
    new_first, new_second, pieces = update(
        limit_sq, squares, mine, fix, first_moment[:, 0], second_moment[:, 0], bases
    )
    pieces = lax.all_to_all(pieces, "dp", 0, 0, tiled=True)
    gate_update, up_update, down_update = layout(pieces)
    return (gate_update.T, up_update.T, down_update, new_first[:, None], new_second[:, None])


def solution(mesh):
    placed = (
        P("dp", None),
        P(None, "dp", "tensor"),
        P("dp", "tensor"),
        P("dp", None),
        P(),
        P(None, "tensor", "dp", None),
        P(None, "tensor", "dp", None),
    )
    return jax.shard_map(
        body,
        mesh=mesh,
        in_specs=placed,
        out_specs=(
            P("dp", "tensor"),
            P("dp", "tensor"),
            P("tensor", "dp"),
            P(None, "tensor", "dp", None),
            P(None, "tensor", "dp", None),
        ),
        check_vma=False,
    )
```

```python
import functools

import jax
import jax.numpy as jnp
from jax import lax
from jax.experimental import pallas as pl
from jax.experimental.pallas import tpu as pltpu
from jax.sharding import PartitionSpec as P

STEP = 10
N_Z, N_X, N_C = 4, 4, 2
N_DP = N_Z * N_X * N_C
UNITS = 86
PAD = 88
LANES = 128
BF16 = jnp.bfloat16
F32 = jnp.float32
MB = 1 << 20


def dp_index(z, x, c):
    return ((z % N_Z) * N_X + (x % N_X)) * N_C + c % N_C


def every_chip():
    return [(z, x, c) for z in range(N_Z) for x in range(N_X) for c in range(N_C)]


CORE_PAIRS = [(dp_index(z, x, c), dp_index(z, x, c + 1)) for z, x, c in every_chip()]


FLIPS = ((1, 3), (3, 1))
FLIP_ORDER = tuple((0, b, a, a ^ b) for a, b in FLIPS)


def along_x(turn):
    return [(dp_index(z, x, c), dp_index(z, x ^ FLIPS[c][turn], c)) for z, x, c in every_chip()]


def along_z(turn):
    return [(dp_index(z, x, c), dp_index(z ^ FLIPS[c][turn], x, c)) for z, x, c in every_chip()]


def direct_x(r):
    return [(dp_index(z, x, c), dp_index(z, x ^ FLIP_ORDER[c][r], c)) for z, x, c in every_chip()]


def direct_z(r):
    return [(dp_index(z, x, c), dp_index(z ^ FLIP_ORDER[c][r], x, c)) for z, x, c in every_chip()]


def my_place():
    me = lax.axis_index("dp")
    z = lax.shift_right_logical(me, 3)
    x = lax.bitwise_and(lax.shift_right_logical(me, 1), 3)
    return z, x, lax.bitwise_and(me, 1)


def my_core():
    return my_place()[2]


def turned(offset):
    return jnp.where(my_core() == 0, lax.bitwise_and(4 - offset, 3), offset)


def flip_order(r):
    return turned(lax.bitwise_xor(r, lax.shift_right_logical(r, 1)))


def rank_of(offset):
    at = turned(offset)
    return lax.bitwise_xor(at, lax.shift_right_logical(at, 1))


VMEM = pl.BlockSpec(memory_space=pltpu.VMEM)
ANY = pl.BlockSpec(memory_space=pl.ANY)


def params(mib, **more):
    return pltpu.CompilerParams(vmem_limit_bytes=mib * MB, **more)


def project_kernel(first, steps, window, x_hbm, b_hbm, kept, sent, x, b, acc, sem_a, sem_b):
    count = acc.shape[0]
    wide = x.shape[1] // steps
    half = kept.shape[2]

    def copies(k):
        at = pl.ds(k * wide, wide)
        yield pltpu.make_async_copy(x_hbm.at[:, at], x.at[:, at], sem_a.at[k])
        for m in range(count):
            yield pltpu.make_async_copy(b_hbm.at[first + m, at], b.at[m, at], sem_b.at[m, k])

    for k in range(window):
        for copy in copies(k):
            copy.start()
    for k in range(steps):
        for copy in copies(k):
            copy.wait()
        if k + window < steps:
            for copy in copies(k + window):
                copy.start()
        at = slice(k * wide, (k + 1) * wide)
        for m in range(count):
            part = jnp.dot(x[:, at], b[m, at], preferred_element_type=F32)
            if k == 0:
                acc[m] = part
            elif k < steps - 1:
                acc[m] += part
            else:
                full = (acc[m] + part).astype(BF16)
                low, high = full[:, :half], full[:, half:]
                lower = my_core() == 0
                kept[m] = jnp.where(lower, low, high)
                sent[m] = jnp.where(lower, high, low)


def project(x, bases, first, count, window):
    tokens, width = x.shape
    rank = bases.shape[2]
    steps = 8
    out = jax.ShapeDtypeStruct((count, tokens, rank // 2), BF16)
    return pl.pallas_call(
        functools.partial(project_kernel, first, steps, window),
        in_specs=[ANY, ANY],
        out_specs=[VMEM] * 2,
        out_shape=[out, out],
        scratch_shapes=[
            pltpu.VMEM((tokens, width), BF16),
            pltpu.VMEM((count, width, rank), BF16),
            pltpu.VMEM((count, tokens, rank), F32),
            pltpu.SemaphoreType.DMA((steps,)),
            pltpu.SemaphoreType.DMA((count, steps)),
        ],
        compiler_params=params(58),
        cost_estimate=pl.CostEstimate(
            flops=2 * count * tokens * rank * width,
            bytes_accessed=2 * (tokens * width + count * width * rank),
            transcendentals=0,
        ),
        name="project",
    )(x, bases)


def collect_kernel(x_first, g, h, mine, theirs, stay, go, terms, cut):
    step = pl.program_id(0)
    _, x0, c0 = my_place()
    block = g.shape[1]

    @pl.when(step == 0)
    def _():
        terms[...] = jnp.zeros(terms.shape, F32)

    for m in range(g.shape[0]):
        terms[m, :block] = jnp.dot(g[m], mine[m], preferred_element_type=F32) + jnp.dot(
            h[m], theirs[m], preferred_element_type=F32
        )
        for x in range(N_X):
            at = rank_of(lax.bitwise_xor(x0, x))
            for c in range(N_C):
                own = lax.bitwise_xor(c0, c)
                d = (x * N_C + c) * UNITS
                both = terms[m, d : d + PAD].astype(BF16)
                cut[at, 2 * m, own] = both[:, :LANES]
                cut[at, 2 * m + 1, own] = both[:, LANES:]
    if x_first:
        stay[:, 0] = cut[:2]
        go[:, 0] = cut[2:]
        return

    @pl.when(step < 2)
    def _():
        stay[0] = cut[...]

    @pl.when(step >= 2)
    def _():
        go[0] = cut[...]


def collect(x_first, g, h, mine, theirs):
    count, units, tokens = g.shape
    half = mine.shape[2]
    block = units // N_Z
    pieces = 2 * count
    array = jax.ShapeDtypeStruct((2, 4, pieces, N_C, PAD, LANES), BF16)
    z_of = lambda i: lax.bitwise_xor(my_place()[0], flip_order(i))
    by_z = pl.BlockSpec((count, block, tokens), lambda i: (0, z_of(i), 0))
    whole = pl.BlockSpec((count, tokens, half), lambda i: (0, 0, 0))
    if x_first:
        out_specs = [pl.BlockSpec((2, 1, pieces, N_C, PAD, LANES), lambda i: (0, i, 0, 0, 0, 0))] * 2
    else:
        shape = (1, 4, pieces, N_C, PAD, LANES)
        out_specs = [
            pl.BlockSpec(shape, lambda i: (jnp.minimum(i, 1), 0, 0, 0, 0, 0)),
            pl.BlockSpec(shape, lambda i: (jnp.maximum(i - 2, 0), 0, 0, 0, 0, 0)),
        ]
    return pl.pallas_call(
        functools.partial(collect_kernel, x_first),
        grid=(N_Z,),
        in_specs=[by_z, by_z, whole, whole],
        out_specs=out_specs,
        scratch_shapes=[
            pltpu.VMEM((count, block + 8, half), F32),
            pltpu.VMEM((4, pieces, N_C, PAD, LANES), BF16),
        ],
        out_shape=[array] * 2,
        compiler_params=params(24),
        cost_estimate=pl.CostEstimate(
            flops=2 * count * 2 * tokens * units * half,
            bytes_accessed=2 * count * units * (2 * tokens + half),
            transcendentals=0,
        ),
        name="collect",
    )(g, h, mine, theirs)


def split_kernel(kept, recv, *outs):
    n = kept.shape[0] // len(outs)
    for i, out in enumerate(outs):
        at = slice(i * n, (i + 1) * n)
        out[...] = (kept[at].astype(F32) + recv[at].astype(F32)).astype(BF16)


def split_sum(kept, recv, parts):
    shape = (kept.shape[0] // parts, *kept.shape[1:])
    return pl.pallas_call(
        split_kernel,
        in_specs=[VMEM] * 2,
        out_specs=[VMEM] * parts,
        out_shape=[jax.ShapeDtypeStruct(shape, BF16)] * parts,
        compiler_params=params(12),
        name="split_sum",
    )(kept, recv)


def owned_kernel(*refs):
    parts, (mine, fix, squares) = refs[:-3], refs[-3:]
    inside = lax.broadcasted_iota(jnp.int32, (PAD, LANES), 0) < UNITS
    total_sq = jnp.zeros((PAD, LANES), F32)
    for m in range(3):
        for half in range(2):
            t, piece = (parts[:4], 2 * m + half) if m < 2 else (parts[4:], half)
            lanes = slice(half * LANES, half * LANES + LANES)
            for c in range(N_C):
                v = sum(u[0, piece, c].astype(F32) for u in t)
                total_sq += jnp.where(inside, v * v, 0.0)
                if c == 0:
                    mine[m, :, lanes] = v
                else:
                    fix[m, :, lanes] = v.astype(BF16)
    row = jnp.sum(total_sq, axis=0, keepdims=True)
    squares[...] = jnp.broadcast_to(row, squares.shape)


def owned_sum(by_x, by_z, peers):
    return pl.pallas_call(
        owned_kernel,
        in_specs=[VMEM] * len((*by_x, *by_z)),
        out_specs=[VMEM] * 3,
        out_shape=[
            jax.ShapeDtypeStruct((3, PAD, 2 * LANES), F32),
            jax.ShapeDtypeStruct((3, PAD, 2 * LANES), BF16),
            jax.ShapeDtypeStruct((peers, LANES), F32),
        ],
        compiler_params=params(12),
        name="owned_sum",
    )(*by_x, *by_z)


def update_kernel(
    limit_sq, squares, mine, recv, first, second, b_hbm, new_first, new_second, out, way, b, sem
):
    step = pl.program_id(0)
    wide = b.shape[2]

    def copy(j):
        return pltpu.make_async_copy(b_hbm.at[:, pl.ds(j * wide, wide)], b.at[j], sem.at[j])

    @pl.when(step == 0)
    def _():
        for j in range(b.shape[0]):
            copy(j).start()
        total = jnp.sum(squares[...])
        clip_limit = jnp.sqrt(jnp.full((1, 1), limit_sq, F32))
        factor = jnp.minimum(1.0, clip_limit / jnp.sqrt(jnp.full((1, 1), total, F32)))
        low = my_core() == 0
        for m in range(3):
            near = mine[m]
            far = recv[m].astype(F32)
            lower = jnp.where(low, near, far)
            upper = jnp.where(low, far, near)
            clipped = jnp.concatenate([lower, upper], axis=1)[:UNITS] * factor
            one = 0.9 * first[m] + 0.1 * clipped
            two = 0.95 * second[m] + 0.05 * clipped * clipped
            new_first[m] = one
            new_second[m] = two
            turn = one / (1.0 - 0.9**STEP) / (jnp.sqrt(two / (1.0 - 0.95**STEP)) + 1e-08)
            padded = jnp.concatenate([turn, jnp.zeros((PAD - UNITS, turn.shape[1]), F32)], axis=0)
            way[m] = padded.astype(BF16)

    copy(step).wait()
    for m in range(3):
        full = lax.dot_general(
            way[m], b[step, m], (((1,), (1,)), ((), ())), preferred_element_type=F32
        ).astype(BF16)
        for n in range(out.shape[0]):
            out[n, m] = full[:, n * LANES : (n + 1) * LANES]


def update(limit_sq, squares, mine, recv, first, second, bases):
    _, width, rank = bases.shape
    steps = 4
    moment = jax.ShapeDtypeStruct((3, UNITS, rank), F32)
    whole = lambda array: pl.BlockSpec(array.shape, lambda i: (0,) * array.ndim)
    inputs = (squares, mine, recv, first, second)
    owners = width // LANES
    return pl.pallas_call(
        functools.partial(update_kernel, limit_sq),
        grid=(steps,),
        in_specs=[whole(t) for t in inputs] + [ANY],
        out_specs=[
            whole(moment),
            whole(moment),
            pl.BlockSpec((owners // steps, 3, PAD, LANES), lambda i: (i, 0, 0, 0)),
        ],
        out_shape=[moment, moment, jax.ShapeDtypeStruct((owners, 3, PAD, LANES), BF16)],
        scratch_shapes=[
            pltpu.VMEM((3, PAD, rank), BF16),
            pltpu.VMEM((steps, 3, width // steps, rank), BF16),
            pltpu.SemaphoreType.DMA((steps,)),
        ],
        compiler_params=params(52),
        name="update",
    )(*inputs, bases)


def layout_kernel(pieces, gate, up, down, rows, done, sem):
    units = N_DP * UNITS
    copies = []
    for m, out in enumerate((gate, up, down)):
        for k in range(N_DP):
            rows[m, k * UNITS : k * UNITS + PAD, :] = pieces[k, m].astype(F32)
        done[m] = rows[m, :units, :].astype(BF16)
        copies.append(pltpu.make_async_copy(done.at[m], out, sem.at[m]))
        copies[-1].start()
    for copy in copies:
        copy.wait()


def layout(pieces):
    units = N_DP * UNITS
    return pl.pallas_call(
        layout_kernel,
        in_specs=[VMEM],
        out_specs=[ANY] * 3,
        out_shape=[jax.ShapeDtypeStruct((units, LANES), BF16)] * 3,
        scratch_shapes=[
            pltpu.VMEM((3, units + 8, LANES), F32),
            pltpu.VMEM((3, units, LANES), BF16),
            pltpu.SemaphoreType.DMA((3,)),
        ],
        compiler_params=params(24),
        name="layout",
    )(pieces)


def body(activations, gate_up_grads, hidden_act, down_out_grad, bases, first_moment, second_moment):
    devices = lax.axis_size("dp") * lax.axis_size("tensor")
    total_units = hidden_act.shape[1] * lax.axis_size("tensor")
    gate_up = jnp.swapaxes(gate_up_grads, 1, 2)
    hidden = hidden_act.T[None]
    gate_up_there = lax.ppermute(gate_up, "dp", CORE_PAIRS)
    kept_two, sent_two = project(activations, bases, 0, 2, 4)
    theirs_two = lax.ppermute(sent_two, "dp", CORE_PAIRS)
    kept_one, sent_one = project(down_out_grad, bases, 2, 1, 8)
    theirs_one = lax.ppermute(sent_one, "dp", CORE_PAIRS)
    kept_two, kept_one, theirs_two, later = lax.optimization_barrier(
        (kept_two, kept_one, theirs_two, hidden)
    )
    hidden_there = lax.ppermute(later, "dp", CORE_PAIRS)
    xa, xb = collect(True, gate_up, gate_up_there, kept_two, theirs_two)
    xr = lax.ppermute(xb, "dp", along_x(0))
    za, zb = collect(False, hidden, hidden_there, kept_one, theirs_one)
    zr = lax.ppermute(zb, "dp", along_z(0))
    za, zb = split_sum(za, zr, 2)
    xa, xb = split_sum(xa, xr, 2)
    zr = lax.ppermute(zb, "dp", along_z(1))
    xr = lax.ppermute(xb, "dp", along_x(1))
    za, zb = split_sum(za[0], zr[0], 2)
    zr = lax.ppermute(zb, "dp", along_x(0))
    za, zb = split_sum(za, zr, 2)
    by_x = split_sum(xa[0], xr[0], 4)
    by_z = [za, lax.ppermute(zb, "dp", along_x(1))]
    by_x = [by_x[0]] + [lax.ppermute(by_x[r], "dp", direct_z(r)) for r in (1, 2, 3)]
    mine, fix, squares = owned_sum(by_x, by_z, devices)
    fix = lax.ppermute(fix, "dp", CORE_PAIRS)
    squares = lax.all_to_all(squares, ("dp", "tensor"), 0, 0, tiled=True)

    limit_sq = float(3 * bases.shape[2] * total_units)
    new_first, new_second, pieces = update(
        limit_sq, squares, mine, fix, first_moment[:, 0], second_moment[:, 0], bases
    )
    pieces = lax.all_to_all(pieces, "dp", 0, 0, tiled=True)
    gate_update, up_update, down_update = layout(pieces)
    return (gate_update.T, up_update.T, down_update, new_first[:, None], new_second[:, None])


def solution(mesh):
    placed = (
        P("dp", None),
        P(None, "dp", "tensor"),
        P("dp", "tensor"),
        P("dp", None),
        P(),
        P(None, "tensor", "dp", None),
        P(None, "tensor", "dp", None),
    )
    return jax.shard_map(
        body,
        mesh=mesh,
        in_specs=placed,
        out_specs=(
            P("dp", "tensor"),
            P("dp", "tensor"),
            P("tensor", "dp"),
            P(None, "tensor", "dp", None),
            P(None, "tensor", "dp", None),
        ),
        check_vma=False,
    )
```
